32 devices in a mesh: grp: 4 (over z), seq: 8 (over y, x, core).
Axes of the slice: x: 2, y: 2, z: 4, core: 2. Of those that a mesh axis runs over, the one named last changes fastest.
Arguments:
- main_query: bfloat16 [8, 128, 2560], P('seq', 'grp'), may hold values from -150 to 150
- main_key: bfloat16 [8, 128, 2560], P('seq', 'grp'), may hold values from -4 to 4
- main_value: bfloat16 [8, 128, 2560], P('seq', 'grp'), may hold values from -240 to 240
- guide_query: bfloat16 [8, 128, 1024], P('seq', None, 'grp'), may hold values from -150 to 150
- guide_key: bfloat16 [8, 128, 1024], P('seq', None, 'grp'), may hold values from -4 to 4
- guide_value: bfloat16 [8, 128, 1024], P('seq', None, 'grp'), may hold values from -240 to 240
- latents: float32 [8, 128, 64], P('seq', 'grp'), may hold values from -6 to 6
- step_index: int32 [1], replicated, may hold values from 0 to 49
- main_mod: bfloat16 [50, 2, 2560], replicated, may hold values from -3 to 3
- guide_mod: bfloat16 [50, 2, 1024], replicated, may hold values from -3 to 3
- main_head: bfloat16 [2560, 64], replicated, may hold values from -0.125 to 0.125
- guide_head: bfloat16 [1024, 64], replicated, may hold values from -0.1875 to 0.1875
Outputs:
- velocity: float32 [8, 128, 64], P('seq', 'grp')
- next_latents: float32 [8, 128, 64], P('seq', 'grp')
The draws below stay inside these ranges and needn't reach their ends.
All inputs are finite; a program needn't handle non-finite values.
Results may differ from the reference program's by a relative error of at most 0.012.
Values may be sent and summed in bfloat16 or wider, within the bound.
A program may use at most 128 MiB of HBM per device.

```python
import math
import jax
import jax.numpy as jnp
from jax import lax

HM = 20
HG = 8
C = 64
STEPS = 50
QM = 2560
QG = 1024
BLOCK = 128
BLOCKS = 8
TOKENS = 1024


def paired_rows(key, salt, width):
    seeded = jax.random.fold_in(key, salt)
    keys_base = jax.random.truncated_normal(jax.random.fold_in(seeded, 1), -4.0, 4.0, (TOKENS, width), jnp.float32)
    queries_base = jax.random.truncated_normal(jax.random.fold_in(seeded, 2), -4.0, 4.0, (TOKENS, width), jnp.float32)
    aligned = jax.random.randint(jax.random.fold_in(seeded, 3), (6,), 0, TOKENS)
    sources = jax.random.randint(jax.random.fold_in(seeded, 4), (6,), 0, TOKENS)
    copies = (sources + 1 + jax.random.randint(jax.random.fold_in(seeded, 5), (6,), 0, TOKENS - 1)) % TOKENS
    queries = queries_base.at[aligned].set(queries_base[aligned])
    keys = keys_base.at[copies].set(keys_base[copies])
    return (queries, keys)


def value_rows(seeded, width, row_spread):
    base = jax.random.truncated_normal(jax.random.fold_in(seeded, 1), -4.0, 4.0, (TOKENS, width), jnp.float32)
    ramp = 3.0 ** (jnp.arange(width, dtype=jnp.float32) / (width - 1))
    column_scale = 3.3 ** jax.random.uniform(jax.random.fold_in(seeded, 2), (width,), jnp.float32)
    row_scale = row_spread ** jax.random.uniform(jax.random.fold_in(seeded, 3), (TOKENS,), jnp.float32)
    return base * ramp[None, :] * column_scale[None, :] * row_scale[:, None]


def draw_main_query(key, part):
    drawn = paired_rows(key, 31, QM)
    return drawn[0].reshape(BLOCKS, BLOCK, QM).astype(jnp.bfloat16)


def draw_main_key(key, part):
    drawn = paired_rows(key, 31, QM)
    return drawn[1].reshape(BLOCKS, BLOCK, QM).astype(jnp.bfloat16)


def draw_guide_query(key, part):
    drawn = paired_rows(key, 47, QG)
    return drawn[0].reshape(BLOCKS, BLOCK, QG).astype(jnp.bfloat16)


def draw_guide_key(key, part):
    drawn = paired_rows(key, 47, QG)
    return drawn[1].reshape(BLOCKS, BLOCK, QG).astype(jnp.bfloat16)


def draw_main_value(key, part):
    key = jax.random.fold_in(key, 7)
    values = value_rows(key, QM, 1.0)
    return values.reshape(BLOCKS, BLOCK, QM).astype(jnp.bfloat16)


def draw_guide_value(key, part):
    key = jax.random.fold_in(key, 9)
    values = value_rows(key, QG, 1.0)
    return values.reshape(BLOCKS, BLOCK, QG).astype(jnp.bfloat16)


def levels(stream_key, extent, pieces, smallest, largest):
    level = 1.0
    for position, parts in pieces:
        draws = jax.random.uniform(jax.random.fold_in(jax.random.fold_in(stream_key, 6), position), (parts,), jnp.float32, smallest / len(pieces), largest / len(pieces))
        level = level * jnp.repeat(jnp.exp(draws), extent[position] // parts).reshape((-1,) + (1,) * (len(extent) - 1 - position))
    return level


def gaussian(stream_key, dims, scale, reach, pieces=(), kind=jnp.bfloat16):
    loudness = levels(stream_key, dims, pieces, -0.22, 0.18) if pieces else 1.0
    values = jax.random.normal(stream_key, dims, jnp.float32) * scale * loudness
    return jnp.minimum(jnp.maximum(values, -reach), reach).astype(kind)


def setup_inputs(seed: int = 0) -> dict:
    key_of = jax.random.split(jax.random.key(seed), 13)
    main_query = draw_main_query(jax.random.fold_in(key_of[12], 71), 0)
    main_key = draw_main_key(jax.random.fold_in(key_of[12], 71), 0)
    main_value = draw_main_value(jax.random.fold_in(key_of[12], 71), 0)
    guide_query = draw_guide_query(jax.random.fold_in(key_of[12], 71), 0)
    guide_key = draw_guide_key(jax.random.fold_in(key_of[12], 71), 0)
    guide_value = draw_guide_value(jax.random.fold_in(key_of[12], 71), 0)
    latents = gaussian(key_of[6], (BLOCKS, BLOCK, C), 1.0, 6.0, ((0, 8), (1, 4)), jnp.float32)
    step_index = jax.random.randint(key_of[7], (1,), 0, STEPS).astype(jnp.int32)
    main_mod = gaussian(key_of[8], (STEPS, 2, QM), 0.5, 3.0)
    guide_mod = gaussian(key_of[9], (STEPS, 2, QG), 0.5, 3.0)
    main_head = gaussian(key_of[10], (QM, C), QM ** -0.5, 0.125)
    guide_head = gaussian(key_of[11], (QG, C), QG ** -0.5, 0.1875)
    return dict(main_query=main_query, main_key=main_key, main_value=main_value, guide_query=guide_query, guide_key=guide_key, guide_value=guide_value, latents=latents, step_index=step_index, main_mod=main_mod, guide_mod=guide_mod, main_head=main_head, guide_head=guide_head)


guidance = 2.5
flow_shift = 3.0
epsilon = 1e-06

def attend(queries, keys, values, heads):
    total = queries.shape[0]
    width = queries.shape[1]
    depth = width // heads
    keys_wide = keys.astype(jnp.float32).reshape(total, heads, depth)
    values_wide = values.astype(jnp.float32).reshape(total, heads, depth)
    block = math.gcd(total, 512)
    grouped = queries.astype(jnp.float32).reshape(total // block, block, heads, depth)
    factor = 1.0 / math.sqrt(depth)

    def one_block(rows_here):
        scores = jnp.einsum('rhd,khd->hrk', rows_here, keys_wide) * factor
        highest = lax.optimization_barrier(jnp.max(scores, axis=-1, keepdims=True))
        weights = jnp.exp(scores - highest)
        weight_sum = lax.optimization_barrier(jnp.sum(weights, axis=-1))
        rounded = lax.optimization_barrier(weights.astype(jnp.bfloat16)).astype(jnp.float32)
        summed = jnp.einsum('hrk,khd->rhd', rounded, values_wide)
        return summed / jnp.transpose(weight_sum)[:, :, None]
    result = lax.map(one_block, grouped)
    return lax.optimization_barrier(result.reshape(total, width).astype(jnp.bfloat16))

def project(attended, table, step_now, weight):
    row_now = lax.dynamic_index_in_dim(table, step_now, 0, keepdims=False).astype(jnp.float32)
    values = attended.astype(jnp.float32)
    center = lax.optimization_barrier(jnp.mean(values, axis=-1, keepdims=True))
    centered = values - center
    spread = lax.optimization_barrier(jnp.mean(centered * centered, axis=-1, keepdims=True))
    normed = centered * lax.rsqrt(spread + epsilon)
    modulated = normed * (1.0 + row_now[1]) + row_now[0]
    return jnp.dot(modulated, weight.astype(jnp.float32), precision=lax.Precision.HIGHEST)

def sigma_at(index):
    remaining = 1.0 - index.astype(jnp.float32) / STEPS
    return flow_shift * remaining / (1.0 + (flow_shift - 1.0) * remaining)

def reference(main_query, main_key, main_value, guide_query, guide_key, guide_value, latents, step_index, main_mod, guide_mod, main_head, guide_head):
    step_now = step_index[0]
    main_out = attend(main_query.reshape(TOKENS, QM), main_key.reshape(TOKENS, QM), main_value.reshape(TOKENS, QM), HM)
    guide_out = attend(guide_query.reshape(TOKENS, QG), guide_key.reshape(TOKENS, QG), guide_value.reshape(TOKENS, QG), HG)
    main_flow = project(main_out, main_mod, step_now, main_head)
    guide_flow = project(guide_out, guide_mod, step_now, guide_head)
    velocity = (guide_flow + guidance * (main_flow - guide_flow)).reshape(latents.shape)
    advanced = latents + (sigma_at(step_now + 1) - sigma_at(step_now)) * velocity
    return (velocity, advanced)
```

```python
import functools
import math

import jax
import jax.numpy as jnp
from jax import lax
from jax.experimental import pallas as pl
from jax.experimental.pallas import tpu as pltpu
from jax.sharding import PartitionSpec as P

HD = 128
HM = 20
STEPS = 50
SLOTS = 8

guidance = 2.5
flow_shift = 3.0
epsilon = 1e-06

KEY, QUERY, VALUE = 0, 1, 2


def sigma_at(index):
    remaining = 1.0 - index.astype(jnp.float32) / STEPS
    return flow_shift * remaining / (1.0 + (flow_shift - 1.0) * remaining)


def aligned(value, multiple):
    return pl.multiple_of(value, multiple)


def wait_for(ref, sem):
    pltpu.make_async_copy(ref, ref, sem).wait()


def loop(count, body):
    if count <= 8:
        for i in range(count):
            body(i)
    else:
        pl.loop(0, count)(body)


def project(pieces, row, weight_ref):
    width = sum(piece.shape[1] for piece in pieces)
    center = sum(jnp.sum(piece, axis=-1, keepdims=True) for piece in pieces) * (1.0 / width)
    centered = [piece - center for piece in pieces]
    spread = sum(jnp.sum(piece * piece, axis=-1, keepdims=True) for piece in centered) * (1.0 / width)
    scale = lax.rsqrt(spread + epsilon)
    total = None
    start = 0
    for piece in centered:
        part = slice(start, start + piece.shape[1])
        start += piece.shape[1]
        wide = piece * scale * (1.0 + row[1:2, part]) + row[0:1, part]
        high = wide.astype(jnp.bfloat16)
        rest = wide - high.astype(jnp.float32)
        middle = rest.astype(jnp.bfloat16)
        low = (rest - middle.astype(jnp.float32)).astype(jnp.bfloat16)
        product = jnp.dot(
            jnp.concatenate([high, middle, low], axis=0),
            weight_ref[part, :],
            preferred_element_type=jnp.float32,
        )
        total = product if total is None else total + product
    rows = total.shape[0] // 3
    return total[:rows] + total[rows : 2 * rows] + total[2 * rows :]


def kernel(
    G, S, R, main_heads, guide_heads,
    step_ref, main_q, main_k, main_v, guide_q, guide_k, guide_v,
    main_mod, guide_mod, main_head, guide_head,
    main_flow, guide_flow,
    moved, keys, queries, values, weights, sums, attended, returned, final,
    main_table, guide_table, main_weight, guide_weight,
    table_sem, z_recv, z_send, p_recv, p_send, o_recv, o_send, f_recv, f_send,
):
    g = lax.axis_index("grp")
    s = lax.axis_index("seq")
    rows = main_q.shape[1]
    block = guide_q.shape[1]
    tokens = keys.shape[0]
    count = queries.shape[0]
    blocks = count // block
    heads = main_heads + guide_heads
    wide = main_heads * HD
    slot = s // R
    part = s % R

    tables = (
        (main_mod, main_table), (guide_mod, guide_table),
        (main_head, main_weight), (guide_head, guide_weight),
    )

    barrier = pltpu.get_barrier_semaphore()
    for d in range(1, G):
        pl.semaphore_signal(barrier, inc=1, device_id={"grp": (g + d) % G})

    def greet(i):
        pl.semaphore_signal(barrier, inc=1, device_id={"seq": (s + 1 + i) % S})

    loop(S - 1, greet)

    sources = (main_k, main_q, main_v)
    my_rows = pl.ds(aligned(g * rows, rows), rows)
    for a in range(3):
        pltpu.make_async_copy(
            sources[a].at[0, :, pl.ds(aligned(g * wide, HD), wide)],
            moved.at[a, my_rows, :],
            z_recv.at[a],
        ).start()

    pl.semaphore_wait(barrier, G - 1 + S - 1)

    def send_z(a):
        for d in range(1, G):
            peer = (g + d) % G
            pltpu.make_async_remote_copy(
                src_ref=sources[a].at[0, :, pl.ds(aligned(peer * wide, HD), wide)],
                dst_ref=moved.at[a, my_rows, :],
                send_sem=z_send,
                recv_sem=z_recv.at[a],
                device_id={"grp": peer},
            ).start()

    targets = (keys, queries, values)

    def plane(a, source, first, number, act):
        def one(index):
            head = (index + s) % number
            src = source.at[:, pl.ds(aligned(head * HD, HD), HD)]
            if a == QUERY:
                dst = targets[a].at[pl.ds(aligned((s % blocks) * block, block), block), :]
            else:
                dst = targets[a].at[pl.ds(aligned(s * block, block), block), :]

            def to(unit):
                act(a, src, dst, unit)

            if a == QUERY:
                to((first + head) * R + s // blocks)
            else:
                loop(R, lambda r: to((first + head) * R + r))

        loop(number, one)

    def start(a, src, dst, unit):
        @pl.when(unit == s)
        def _():
            pltpu.make_async_copy(src, dst, p_recv.at[a]).start()

        @pl.when(unit != s)
        def _():
            pltpu.make_async_remote_copy(
                src_ref=src, dst_ref=dst, send_sem=p_send, recv_sem=p_recv.at[a],
                device_id={"seq": unit},
            ).start()

    def sent(a, src, dst, unit):
        @pl.when(unit != s)
        def _():
            wait_for(dst, p_send)

    guide_sources = (guide_k.at[0], guide_q.at[0], guide_v.at[0])
    send_z(KEY)
    plane(KEY, guide_sources[KEY], main_heads, guide_heads, start)
    send_z(QUERY)
    plane(QUERY, guide_sources[QUERY], main_heads, guide_heads, start)
    send_z(VALUE)
    plane(VALUE, guide_sources[VALUE], main_heads, guide_heads, start)
    for i, (src, dst) in enumerate(tables):
        pltpu.make_async_copy(src, dst, table_sem.at[i]).start()
    for a in range(3):
        wait_for(moved.at[a], z_recv.at[a])
        plane(a, moved.at[a], 0, main_heads, start)

    factor = math.log2(math.e) / math.sqrt(HD)
    score_rows = max(32, min(256, 256 * 1024 // tokens))
    value_rows = min(256, count)

    @pl.when(slot < heads)
    def _():
        wait_for(keys, p_recv.at[KEY])
        wait_for(queries, p_recv.at[QUERY])

        def score(i):
            at = pl.ds(i * score_rows, score_rows)
            scores = lax.dot_general(
                queries[at, :], keys[...], (((1,), (1,)), ((), ())),
                preferred_element_type=jnp.float32,
            )
            highest = jnp.max(scores, axis=-1, keepdims=True)
            unrounded = jnp.exp2((scores - highest) * factor)
            sums[at, :] = jnp.broadcast_to(
                jnp.sum(unrounded, axis=-1, keepdims=True), (score_rows, HD)
            )
            weights[at, :] = unrounded.astype(jnp.bfloat16)

        loop(count // score_rows, score)
        wait_for(values, p_recv.at[VALUE])
        columns = pl.ds(aligned(slot * HD, HD), HD)
        for i in range(count // value_rows):
            at = pl.ds(i * value_rows, value_rows)
            summed = jnp.dot(weights[at, :], values[...], preferred_element_type=jnp.float32)
            attended[at, :] = (summed / sums[at, :]).astype(jnp.bfloat16)
            for b in range(i * value_rows // block, (i + 1) * value_rows // block):
                src = attended.at[pl.ds(b * block, block), :]
                dst = returned.at[:, columns]
                owner = part * blocks + b

                @pl.when(owner == s)
                def _():
                    pltpu.make_async_copy(src, dst, o_recv).start()

                @pl.when(owner != s)
                def _():
                    pltpu.make_async_remote_copy(
                        src_ref=src, dst_ref=dst, send_sem=o_send, recv_sem=o_recv,
                        device_id={"seq": owner},
                    ).start()

    wait_for(returned, o_recv)
    pltpu.make_async_copy(returned.at[my_rows, :], final.at[g], f_recv).start()
    for d in range(1, G):
        peer = (g + d) % G
        pltpu.make_async_remote_copy(
            src_ref=returned.at[pl.ds(aligned(peer * rows, rows), rows), :],
            dst_ref=final.at[g],
            send_sem=f_send,
            recv_sem=f_recv,
            device_id={"grp": peer},
        ).start()

    for a in range(3):
        wait_for(moved.at[a, pl.ds(0, (G - 1) * rows), :], z_send)
        plane(a, guide_sources[a], main_heads, guide_heads, sent)
        plane(a, moved.at[a], 0, main_heads, sent)

    @pl.when(slot < heads)
    def _():
        for b in range(blocks):
            @pl.when(part * blocks + b != s)
            def _():
                wait_for(attended.at[pl.ds(b * block, block), :], o_send)

    for i, (src, dst) in enumerate(tables):
        pltpu.make_async_copy(src, dst, table_sem.at[i]).wait()
    step_now = step_ref[0]
    main_row = main_table[step_now].astype(jnp.float32)
    guide_row = guide_table[step_now].astype(jnp.float32)
    wait_for(final, f_recv)
    main_flow[...] = project(
        [final[i, :, :wide].astype(jnp.float32) for i in range(G)], main_row, main_weight
    )
    guide_flow[...] = project(
        [final[i, :, wide:].astype(jnp.float32) for i in range(G)], guide_row, guide_weight
    )
    wait_for(final.at[pl.ds(0, G - 1)], f_send)


def on_device(G, S, *arguments):
    (main_query, main_key, main_value, guide_query, guide_key, guide_value,
     latents, step_index, main_mod, guide_mod, main_head, guide_head) = arguments
    R = max(1, S // SLOTS)
    main_heads = HM // G
    guide_heads = guide_query.shape[2] // HD
    heads = main_heads + guide_heads
    rows = main_query.shape[1]
    block = guide_query.shape[1]
    tokens = S * block
    count = tokens // R
    channels = main_head.shape[1]
    bf16 = jnp.bfloat16
    anywhere = pl.BlockSpec(memory_space=pl.ANY)
    vmem = pl.BlockSpec(memory_space=pltpu.VMEM)
    dma = pltpu.SemaphoreType.DMA
    main_flow, guide_flow = pl.pallas_call(
        functools.partial(kernel, G, S, R, main_heads, guide_heads),
        out_shape=[jax.ShapeDtypeStruct((rows, channels), jnp.float32)] * 2,
        in_specs=[pl.BlockSpec(memory_space=pltpu.SMEM)] + [anywhere] * 10,
        out_specs=[vmem, vmem],
        scratch_shapes=[
            pltpu.VMEM((3, block, main_heads * HD), bf16),
            pltpu.VMEM((tokens, HD), bf16),
            pltpu.VMEM((count, HD), bf16),
            pltpu.VMEM((tokens, HD), bf16),
            pltpu.VMEM((count, tokens), bf16),
            pltpu.VMEM((count, HD), jnp.float32),
            pltpu.VMEM((count, HD), bf16),
            pltpu.VMEM((block, heads * HD), bf16),
            pltpu.VMEM((G, rows, heads * HD), bf16),
            pltpu.VMEM(main_mod.shape, bf16),
            pltpu.VMEM(guide_mod.shape, bf16),
            pltpu.VMEM(main_head.shape, bf16),
            pltpu.VMEM(guide_head.shape, bf16),
            dma((4,)), dma((3,)), dma, dma((3,)), dma, dma, dma, dma, dma,
        ],
        compiler_params=pltpu.CompilerParams(
            collective_id=0, has_side_effects=True, vmem_limit_bytes=48 * 1024 * 1024
        ),
        cost_estimate=pl.CostEstimate(
            flops=4 * count * tokens * HD, bytes_accessed=4 * tokens * HD * 2,
            transcendentals=count * tokens,
        ),
    )(
        step_index, main_query, main_key, main_value, guide_query, guide_key, guide_value,
        main_mod, guide_mod, main_head, guide_head,
    )
    step_now = step_index[0]
    velocity = (guide_flow + guidance * (main_flow - guide_flow))[None]
    advanced = latents + (sigma_at(step_now + 1) - sigma_at(step_now)) * velocity
    return (velocity, advanced)


def solution(mesh):
    return jax.shard_map(
        functools.partial(on_device, mesh.shape["grp"], mesh.shape["seq"]),
        mesh=mesh,
        in_specs=(
            P("seq", "grp", None),
            P("seq", "grp", None),
            P("seq", "grp", None),
            P("seq", None, "grp"),
            P("seq", None, "grp"),
            P("seq", None, "grp"),
            P("seq", "grp", None),
            P(),
            P(),
            P(),
            P(),
            P(),
        ),
        out_specs=(P("seq", "grp", None), P("seq", "grp", None)),
        check_vma=False,
    )
```

```python
import functools
import math

import jax
import jax.numpy as jnp
from jax import lax
from jax.experimental import pallas as pl
from jax.experimental.pallas import tpu as pltpu
from jax.sharding import PartitionSpec as P

HD = 128
HM = 20
STEPS = 50
SLOTS = 8

guidance = 2.5
flow_shift = 3.0
epsilon = 1e-06

KEY, QUERY, VALUE = 0, 1, 2


def sigma_at(index):
    remaining = 1.0 - index.astype(jnp.float32) / STEPS
    return flow_shift * remaining / (1.0 + (flow_shift - 1.0) * remaining)


def aligned(value, multiple):
    return pl.multiple_of(value, multiple)


def wait_for(ref, sem):
    pltpu.make_async_copy(ref, ref, sem).wait()


def loop(count, body):
    if count <= 8:
        for i in range(count):
            body(i)
    else:
        pl.loop(0, count)(body)


def project(pieces, row, weight_ref):
    width = sum(piece.shape[1] for piece in pieces)
    center = sum(jnp.sum(piece, axis=-1, keepdims=True) for piece in pieces) * (1.0 / width)
    centered = [piece - center for piece in pieces]
    spread = sum(jnp.sum(piece * piece, axis=-1, keepdims=True) for piece in centered) * (1.0 / width)
    scale = lax.rsqrt(spread + epsilon)
    total = None
    start = 0
    for piece in centered:
        part = slice(start, start + piece.shape[1])
        start += piece.shape[1]
        wide = piece * scale * (1.0 + row[1:2, part]) + row[0:1, part]
        high = wide.astype(jnp.bfloat16)
        rest = wide - high.astype(jnp.float32)
        middle = rest.astype(jnp.bfloat16)
        low = (rest - middle.astype(jnp.float32)).astype(jnp.bfloat16)
        product = lax.dot_general(
            jnp.concatenate([high, middle, low], axis=0),
            weight_ref[:, part],
            (((1,), (1,)), ((), ())),
            preferred_element_type=jnp.float32,
        )
        total = product if total is None else total + product
    rows = total.shape[0] // 3
    return total[:rows] + total[rows : 2 * rows] + total[2 * rows :]


def kernel(
    G, S, R, main_heads, guide_heads,
    step_ref, main_q, main_k, main_v, guide_q, guide_k, guide_v,
    main_mod, guide_mod, main_head, guide_head, latents,
    velocity, advanced,
    moved, keys, queries, values, weights, sums, attended, returned, final,
    main_table, guide_table, main_weight, guide_weight, held_latents,
    table_sem, z_recv, z_send, p_recv, p_send, o_recv, o_send, f_recv, f_send,
):
    g = lax.axis_index("grp")
    s = lax.axis_index("seq")
    rows = main_q.shape[1]
    block = guide_q.shape[1]
    tokens = keys.shape[0]
    count = queries.shape[0]
    blocks = count // block
    heads = main_heads + guide_heads
    wide = main_heads * HD
    slot = s // R
    part = s % R

    tables = (
        (main_mod, main_table), (guide_mod, guide_table),
        (main_head, main_weight), (guide_head, guide_weight),
        (latents, held_latents),
    )

    barrier = pltpu.get_barrier_semaphore()
    for d in range(1, G):
        pl.semaphore_signal(barrier, inc=1, device_id={"grp": (g + d) % G})

    def greet(i):
        pl.semaphore_signal(barrier, inc=1, device_id={"seq": (s + 1 + i) % S})

    loop(S - 1, greet)

    sources = (main_k, main_q, main_v)
    my_rows = pl.ds(aligned(g * rows, rows), rows)
    for a in range(3):
        pltpu.make_async_copy(
            sources[a].at[0, :, pl.ds(aligned(g * wide, HD), wide)],
            moved.at[a, my_rows, :],
            z_recv.at[a],
        ).start()

    pl.semaphore_wait(barrier, G - 1 + S - 1)

    def send_z(a):
        for d in range(1, G):
            peer = (g + d) % G
            pltpu.make_async_remote_copy(
                src_ref=sources[a].at[0, :, pl.ds(aligned(peer * wide, HD), wide)],
                dst_ref=moved.at[a, my_rows, :],
                send_sem=z_send,
                recv_sem=z_recv.at[a],
                device_id={"grp": peer},
            ).start()

    targets = (keys, queries, values)

    def plane(a, source, first, number, act):
        def one(index):
            head = (index + s) % number
            src = source.at[:, pl.ds(aligned(head * HD, HD), HD)]
            if a == QUERY:
                dst = targets[a].at[pl.ds(aligned((s % blocks) * block, block), block), :]
            else:
                dst = targets[a].at[pl.ds(aligned(s * block, block), block), :]

            def to(unit):
                act(a, src, dst, unit)

            if a == QUERY:
                to((first + head) * R + s // blocks)
            else:
                loop(R, lambda r: to((first + head) * R + r))

        loop(number, one)

    def start(a, src, dst, unit):
        @pl.when(unit == s)
        def _():
            pltpu.make_async_copy(src, dst, p_recv.at[a]).start()

        @pl.when(unit != s)
        def _():
            pltpu.make_async_remote_copy(
                src_ref=src, dst_ref=dst, send_sem=p_send, recv_sem=p_recv.at[a],
                device_id={"seq": unit},
            ).start()

    def sent(a, src, dst, unit):
        @pl.when(unit != s)
        def _():
            wait_for(dst, p_send)

    guide_sources = (guide_k.at[0], guide_q.at[0], guide_v.at[0])
    send_z(KEY)
    plane(KEY, guide_sources[KEY], main_heads, guide_heads, start)
    send_z(QUERY)
    plane(QUERY, guide_sources[QUERY], main_heads, guide_heads, start)
    send_z(VALUE)
    plane(VALUE, guide_sources[VALUE], main_heads, guide_heads, start)
    for i, (src, dst) in enumerate(tables):
        pltpu.make_async_copy(src, dst, table_sem.at[i]).start()
    for a in range(3):
        wait_for(moved.at[a], z_recv.at[a])
        plane(a, moved.at[a], 0, main_heads, start)

    factor = math.log2(math.e) / math.sqrt(HD)
    score_rows = max(32, min(256, 256 * 1024 // tokens))
    value_rows = min(256, count)

    @pl.when(slot < heads)
    def _():
        wait_for(keys, p_recv.at[KEY])
        wait_for(queries, p_recv.at[QUERY])

        def score(i):
            at = pl.ds(i * score_rows, score_rows)
            scores = lax.dot_general(
                queries[at, :], keys[...], (((1,), (1,)), ((), ())),
                preferred_element_type=jnp.float32,
            )
            highest = jnp.max(scores, axis=-1, keepdims=True)
            unrounded = jnp.exp2((scores - highest) * factor)
            sums[at, :] = jnp.broadcast_to(
                jnp.sum(unrounded, axis=-1, keepdims=True), (score_rows, HD)
            )
            weights[at, :] = unrounded.astype(jnp.bfloat16)

        loop(count // score_rows, score)
        wait_for(values, p_recv.at[VALUE])
        columns = pl.ds(aligned(slot * HD, HD), HD)
        for i in range(count // value_rows):
            at = pl.ds(i * value_rows, value_rows)
            summed = jnp.dot(weights[at, :], values[...], preferred_element_type=jnp.float32)
            attended[at, :] = (summed / sums[at, :]).astype(jnp.bfloat16)
            for b in range(i * value_rows // block, (i + 1) * value_rows // block):
                src = attended.at[pl.ds(b * block, block), :]
                dst = returned.at[:, columns]
                owner = part * blocks + b

                @pl.when(owner == s)
                def _():
                    pltpu.make_async_copy(src, dst, o_recv).start()

                @pl.when(owner != s)
                def _():
                    pltpu.make_async_remote_copy(
                        src_ref=src, dst_ref=dst, send_sem=o_send, recv_sem=o_recv,
                        device_id={"seq": owner},
                    ).start()

    wait_for(returned, o_recv)
    pltpu.make_async_copy(returned.at[my_rows, :], final.at[g], f_recv).start()
    for d in range(1, G):
        peer = (g + d) % G
        pltpu.make_async_remote_copy(
            src_ref=returned.at[pl.ds(aligned(peer * rows, rows), rows), :],
            dst_ref=final.at[g],
            send_sem=f_send,
            recv_sem=f_recv,
            device_id={"grp": peer},
        ).start()

    for a in range(3):
        wait_for(moved.at[a, pl.ds(0, (G - 1) * rows), :], z_send)
        plane(a, guide_sources[a], main_heads, guide_heads, sent)
        plane(a, moved.at[a], 0, main_heads, sent)

    @pl.when(slot < heads)
    def _():
        for b in range(blocks):
            @pl.when(part * blocks + b != s)
            def _():
                wait_for(attended.at[pl.ds(b * block, block), :], o_send)

    for i, (src, dst) in enumerate(tables):
        pltpu.make_async_copy(src, dst, table_sem.at[i]).wait()
    step_now = step_ref[0]
    main_row = main_table[step_now].astype(jnp.float32)
    guide_row = guide_table[step_now].astype(jnp.float32)
    wait_for(final, f_recv)
    main_flow = project(
        [final[i, :, :wide].astype(jnp.float32) for i in range(G)], main_row, main_weight
    )
    guide_flow = project(
        [final[i, :, wide:].astype(jnp.float32) for i in range(G)], guide_row, guide_weight
    )
    mixed = guide_flow + guidance * (main_flow - guide_flow)
    index = jnp.full((1, mixed.shape[1]), step_now, jnp.int32)
    velocity[0] = mixed
    advanced[0] = held_latents[0] + (sigma_at(index + 1) - sigma_at(index)) * mixed
    wait_for(final.at[pl.ds(0, G - 1)], f_send)


def on_device(G, S, *arguments):
    (main_query, main_key, main_value, guide_query, guide_key, guide_value,
     latents, step_index, main_mod, guide_mod, main_head, guide_head) = arguments
    R = max(1, S // SLOTS)
    main_heads = HM // G
    guide_heads = guide_query.shape[2] // HD
    heads = main_heads + guide_heads
    rows = main_query.shape[1]
    block = guide_query.shape[1]
    tokens = S * block
    count = tokens // R
    bf16 = jnp.bfloat16
    anywhere = pl.BlockSpec(memory_space=pltpu.HBM)
    vmem = pl.BlockSpec(memory_space=pltpu.VMEM)
    dma = pltpu.SemaphoreType.DMA
    return pl.pallas_call(
        functools.partial(kernel, G, S, R, main_heads, guide_heads),
        out_shape=[jax.ShapeDtypeStruct(latents.shape, jnp.float32)] * 2,
        in_specs=[pl.BlockSpec(memory_space=pltpu.SMEM)] + [anywhere] * 11,
        out_specs=[vmem, vmem],
        scratch_shapes=[
            pltpu.VMEM((3, block, main_heads * HD), bf16),
            pltpu.VMEM((tokens, HD), bf16),
            pltpu.VMEM((count, HD), bf16),
            pltpu.VMEM((tokens, HD), bf16),
            pltpu.VMEM((count, tokens), bf16),
            pltpu.VMEM((count, HD), jnp.float32),
            pltpu.VMEM((count, HD), bf16),
            pltpu.VMEM((block, heads * HD), bf16),
            pltpu.VMEM((G, rows, heads * HD), bf16),
            pltpu.VMEM(main_mod.shape, bf16),
            pltpu.VMEM(guide_mod.shape, bf16),
            pltpu.VMEM(main_head.shape[::-1], bf16),
            pltpu.VMEM(guide_head.shape[::-1], bf16),
            pltpu.VMEM(latents.shape, jnp.float32),
            dma((5,)), dma((3,)), dma, dma((3,)), dma, dma, dma, dma, dma,
        ],
        compiler_params=pltpu.CompilerParams(
            collective_id=0, has_side_effects=True, vmem_limit_bytes=60 * 1024 * 1024
        ),
        cost_estimate=pl.CostEstimate(
            flops=4 * count * tokens * HD, bytes_accessed=4 * tokens * HD * 2,
            transcendentals=count * tokens,
        ),
    )(
        step_index, main_query, main_key, main_value, guide_query, guide_key, guide_value,
        main_mod, guide_mod, main_head.T, guide_head.T, latents,
    )


def solution(mesh):
    return jax.shard_map(
        functools.partial(on_device, mesh.shape["grp"], mesh.shape["seq"]),
        mesh=mesh,
        in_specs=(
            P("seq", "grp", None),
            P("seq", "grp", None),
            P("seq", "grp", None),
            P("seq", None, "grp"),
            P("seq", None, "grp"),
            P("seq", None, "grp"),
            P("seq", "grp", None),
            P(),
            P(),
            P(),
            P(),
            P(),
        ),
        out_specs=(P("seq", "grp", None), P("seq", "grp", None)),
        check_vma=False,
    )
```

```python
import functools
import math

import jax
import jax.numpy as jnp
from jax import lax
from jax.experimental import pallas as pl
from jax.experimental.pallas import tpu as pltpu
from jax.sharding import PartitionSpec as P

HD = 128
HM = 20
STEPS = 50
SLOTS = 8

guidance = 2.5
flow_shift = 3.0
epsilon = 1e-06

KEY, QUERY, VALUE = 0, 1, 2


def sigma_at(index):
    remaining = 1.0 - index.astype(jnp.float32) / STEPS
    return flow_shift * remaining / (1.0 + (flow_shift - 1.0) * remaining)


def aligned(value, multiple):
    return pl.multiple_of(value, multiple)


def wait_for(ref, sem):
    pltpu.make_async_copy(ref, ref, sem).wait()


def loop(count, body):
    if count <= 8:
        for i in range(count):
            body(i)
    else:
        pl.loop(0, count)(body)


def project(pieces, row, weight_ref):
    width = sum(piece.shape[1] for piece in pieces)
    center = sum(jnp.sum(piece, axis=-1, keepdims=True) for piece in pieces) * (1.0 / width)
    centered = [piece - center for piece in pieces]
    spread = sum(jnp.sum(piece * piece, axis=-1, keepdims=True) for piece in centered) * (1.0 / width)
    scale = lax.rsqrt(spread + epsilon)
    total = None
    start = 0
    for piece in centered:
        part = slice(start, start + piece.shape[1])
        start += piece.shape[1]
        wide = piece * scale * (1.0 + row[1:2, part]) + row[0:1, part]
        high = wide.astype(jnp.bfloat16)
        rest = wide - high.astype(jnp.float32)
        middle = rest.astype(jnp.bfloat16)
        low = (rest - middle.astype(jnp.float32)).astype(jnp.bfloat16)
        product = lax.dot_general(
            jnp.concatenate([high, middle, low], axis=0),
            weight_ref[:, part],
            (((1,), (1,)), ((), ())),
            preferred_element_type=jnp.float32,
        )
        total = product if total is None else total + product
    rows = total.shape[0] // 3
    return total[:rows] + total[rows : 2 * rows] + total[2 * rows :]


def kernel(
    G, S, R, main_heads, guide_heads,
    step_ref, main_q, main_k, main_v, guide_q, guide_k, guide_v,
    main_mod, guide_mod, main_head, guide_head, latents,
    velocity, advanced,
    keys, queries, values, weights, sums, attended, final,
    main_table, guide_table, main_weight, guide_weight, held_latents,
    table_sem, recv, send, o_recv, o_send,
):
    g = lax.axis_index("grp")
    s = lax.axis_index("seq")
    rows = main_q.shape[1]
    block = guide_q.shape[1]
    tokens = keys.shape[0]
    count = queries.shape[0]
    blocks = count // block
    heads = main_heads + guide_heads
    half = SLOTS // 2
    unit = (s + 2 * R * g * (S - 1)) % S
    slot = unit // R
    part = unit % R
    head_here = slot // 2 + half * (slot % 2)

    def owner(plane, head, r):
        place = (2 * head) % SLOTS + head // half
        return (place * R + r + 2 * R * plane) % S

    tables = (
        (main_mod, main_table), (guide_mod, guide_table),
        (main_head, main_weight), (guide_head, guide_weight),
        (latents, held_latents),
    )

    barrier = pltpu.get_barrier_semaphore()

    def greet(i):
        pl.semaphore_signal(
            barrier, inc=1,
            device_id={"grp": (g + (i + 1) // S) % G, "seq": (s + (i + 1) % S) % S},
        )

    loop(G * S - 1, greet)
    pl.semaphore_wait(barrier, G * S - 1)

    main_sources = (main_k.at[0], main_q.at[0], main_v.at[0])
    guide_sources = (guide_k.at[0], guide_q.at[0], guide_v.at[0])
    targets = (keys, queries, values)

    def spread(a, src, dst, plane, head, act):
        if a == QUERY:
            act(a, src, dst, plane, owner(plane, head, s // blocks))
        else:
            loop(R, lambda r: act(a, src, dst, plane, owner(plane, head, r)))

    def place(a):
        return (s % blocks) * block if a == QUERY else s * block

    def main_pieces(a, act):
        number = G * main_heads

        @pl.loop(0, number)
        def _(i):
            column = (i + (g + 1) * main_heads + s) % number
            src = main_sources[a].at[:, pl.ds(aligned(column * HD, HD), HD)]
            dst = targets[a].at[pl.ds(aligned(place(a) + g * rows, rows), rows), :]
            spread(a, src, dst, column // main_heads, column % main_heads, act)

    def guide_pieces(a, act):
        for i in range(guide_heads):
            head = (i + s) % guide_heads
            src = guide_sources[a].at[:, pl.ds(aligned(head * HD, HD), HD)]
            dst = targets[a].at[pl.ds(aligned(place(a), block), block), :]
            spread(a, src, dst, g, main_heads + head, act)

    def start(a, src, dst, plane, seq):
        here = (plane == g) & (seq == s)

        @pl.when(here)
        def _():
            pltpu.make_async_copy(src, dst, recv.at[a]).start()

        @pl.when(jnp.logical_not(here))
        def _():
            pltpu.make_async_remote_copy(
                src_ref=src, dst_ref=dst, send_sem=send, recv_sem=recv.at[a],
                device_id={"grp": plane, "seq": seq},
            ).start()

    def sent(a, src, dst, plane, seq):
        @pl.when(jnp.logical_not((plane == g) & (seq == s)))
        def _():
            wait_for(dst, send)

    for a in range(3):
        main_pieces(a, start)
        guide_pieces(a, start)
    for i, (src, dst) in enumerate(tables):
        pltpu.make_async_copy(src, dst, table_sem.at[i]).start()

    factor = math.log2(math.e) / math.sqrt(HD)
    score_rows = max(32, min(256, 256 * 1024 // tokens))
    value_rows = min(256, count)
    value_blocks = count // value_rows

    @pl.when(head_here < heads)
    def _():
        wait_for(keys, recv.at[KEY])
        wait_for(queries, recv.at[QUERY])

        def score(i):
            at = pl.ds(i * score_rows, score_rows)
            scores = lax.dot_general(
                queries[at, :], keys[...], (((1,), (1,)), ((), ())),
                preferred_element_type=jnp.float32,
            )
            highest = jnp.max(scores, axis=-1, keepdims=True)
            unrounded = jnp.exp2((scores - highest) * factor)
            sums[at, :] = jnp.broadcast_to(
                jnp.sum(unrounded, axis=-1, keepdims=True), (score_rows, HD)
            )
            weights[at, :] = unrounded.astype(jnp.bfloat16)

        loop(count // score_rows, score)
        wait_for(values, recv.at[VALUE])
        column = aligned((g * heads + head_here) * HD, HD)
        for i in range(value_blocks):
            turn = (i + s // 2) % value_blocks
            at = pl.ds(aligned(turn * value_rows, value_rows), value_rows)
            summed = jnp.dot(weights[at, :], values[...], preferred_element_type=jnp.float32)
            attended[at, :] = (summed / sums[at, :]).astype(jnp.bfloat16)
            for b in range(value_rows // block):
                seq = part * blocks + turn * (value_rows // block) + b
                for d in range(G):
                    plane = (g + d + 1) % G
                    first = turn * value_rows + b * block + plane * rows
                    src = attended.at[pl.ds(aligned(first, rows), rows), :]
                    dst = final.at[:, pl.ds(column, HD)]

                    def send_out():
                        pltpu.make_async_remote_copy(
                            src_ref=src, dst_ref=dst, send_sem=o_send, recv_sem=o_recv,
                            device_id={"grp": plane, "seq": seq},
                        ).start()

                    if d < G - 1:
                        send_out()
                    else:
                        @pl.when(seq == s)
                        def _():
                            pltpu.make_async_copy(src, dst, o_recv).start()

                        pl.when(seq != s)(send_out)

    for a in range(3):
        main_pieces(a, sent)
        guide_pieces(a, sent)
    for i, (src, dst) in enumerate(tables):
        pltpu.make_async_copy(src, dst, table_sem.at[i]).wait()
    step_now = step_ref[0]
    main_row = main_table[step_now].astype(jnp.float32)
    guide_row = guide_table[step_now].astype(jnp.float32)
    wait_for(final, o_recv)

    def taken(first, number):
        return [
            final[:, (i * heads + first) * HD : (i * heads + first + number) * HD].astype(jnp.float32)
            for i in range(G)
        ]

    main_flow = project(taken(0, main_heads), main_row, main_weight)
    guide_flow = project(taken(main_heads, guide_heads), guide_row, guide_weight)
    mixed = guide_flow + guidance * (main_flow - guide_flow)
    index = jnp.full((1, mixed.shape[1]), step_now, jnp.int32)
    velocity[0] = mixed
    advanced[0] = held_latents[0] + (sigma_at(index + 1) - sigma_at(index)) * mixed

    @pl.when(head_here < heads)
    def _():
        wait_for(attended.at[pl.ds(0, count - rows), :], o_send)

        @pl.when(s // blocks != part)
        def _():
            wait_for(attended.at[pl.ds(0, rows), :], o_send)


def on_device(G, S, *arguments):
    (main_query, main_key, main_value, guide_query, guide_key, guide_value,
     latents, step_index, main_mod, guide_mod, main_head, guide_head) = arguments
    R = max(1, S // SLOTS)
    main_heads = HM // G
    guide_heads = guide_query.shape[2] // HD
    heads = main_heads + guide_heads
    rows = main_query.shape[1]
    block = guide_query.shape[1]
    tokens = S * block
    count = tokens // R
    bf16 = jnp.bfloat16
    anywhere = pl.BlockSpec(memory_space=pltpu.HBM)
    vmem = pl.BlockSpec(memory_space=pltpu.VMEM)
    dma = pltpu.SemaphoreType.DMA
    return pl.pallas_call(
        functools.partial(kernel, G, S, R, main_heads, guide_heads),
        out_shape=[jax.ShapeDtypeStruct(latents.shape, jnp.float32)] * 2,
        in_specs=[pl.BlockSpec(memory_space=pltpu.SMEM)] + [anywhere] * 11,
        out_specs=[vmem, vmem],
        scratch_shapes=[
            pltpu.VMEM((tokens, HD), bf16),
            pltpu.VMEM((count, HD), bf16),
            pltpu.VMEM((tokens, HD), bf16),
            pltpu.VMEM((count, tokens), bf16),
            pltpu.VMEM((count, HD), jnp.float32),
            pltpu.VMEM((count, HD), bf16),
            pltpu.VMEM((rows, G * heads * HD), bf16),
            pltpu.VMEM(main_mod.shape, bf16),
            pltpu.VMEM(guide_mod.shape, bf16),
            pltpu.VMEM(main_head.shape[::-1], bf16),
            pltpu.VMEM(guide_head.shape[::-1], bf16),
            pltpu.VMEM(latents.shape, jnp.float32),
            dma((5,)), dma((3,)), dma, dma, dma,
        ],
        compiler_params=pltpu.CompilerParams(
            collective_id=0, has_side_effects=True, vmem_limit_bytes=60 * 1024 * 1024
        ),
        cost_estimate=pl.CostEstimate(
            flops=4 * count * tokens * HD, bytes_accessed=4 * tokens * HD * 2,
            transcendentals=count * tokens,
        ),
    )(
        step_index, main_query, main_key, main_value, guide_query, guide_key, guide_value,
        main_mod, guide_mod, main_head.T, guide_head.T, latents,
    )


def solution(mesh):
    return jax.shard_map(
        functools.partial(on_device, mesh.shape["grp"], mesh.shape["seq"]),
        mesh=mesh,
        in_specs=(
            P("seq", "grp", None),
            P("seq", "grp", None),
            P("seq", "grp", None),
            P("seq", None, "grp"),
            P("seq", None, "grp"),
            P("seq", None, "grp"),
            P("seq", "grp", None),
            P(),
            P(),
            P(),
            P(),
            P(),
        ),
        out_specs=(P("seq", "grp", None), P("seq", "grp", None)),
        check_vma=False,
    )
```

```python
import functools
import math

import jax
import jax.numpy as jnp
from jax import lax
from jax.experimental import pallas as pl
from jax.experimental.pallas import tpu as pltpu
from jax.sharding import PartitionSpec as P

HD = 128
HM = 20
STEPS = 50
SLOTS = 8

guidance = 2.5
flow_shift = 3.0
epsilon = 1e-06

KEY, QUERY, VALUE = 0, 1, 2


def sigma_at(index):
    remaining = 1.0 - index.astype(jnp.float32) / STEPS
    return flow_shift * remaining / (1.0 + (flow_shift - 1.0) * remaining)


def aligned(value, multiple):
    return pl.multiple_of(value, multiple)


def wait_for(ref, sem):
    pltpu.make_async_copy(ref, ref, sem).wait()


def loop(count, body):
    if count <= 8:
        for i in range(count):
            body(i)
    else:
        pl.loop(0, count)(body)


def project(pieces, row, weight_ref):
    width = sum(piece.shape[1] for piece in pieces)
    center = sum(jnp.sum(piece, axis=-1, keepdims=True) for piece in pieces) * (1.0 / width)
    centered = [piece - center for piece in pieces]
    spread = sum(jnp.sum(piece * piece, axis=-1, keepdims=True) for piece in centered) * (1.0 / width)
    scale = lax.rsqrt(spread + epsilon)
    total = None
    start = 0
    for piece in centered:
        part = slice(start, start + piece.shape[1])
        start += piece.shape[1]
        wide = piece * scale * (1.0 + row[1:2, part]) + row[0:1, part]
        high = wide.astype(jnp.bfloat16)
        rest = wide - high.astype(jnp.float32)
        middle = rest.astype(jnp.bfloat16)
        low = (rest - middle.astype(jnp.float32)).astype(jnp.bfloat16)
        product = lax.dot_general(
            jnp.concatenate([high, middle, low], axis=0),
            weight_ref[:, part],
            (((1,), (1,)), ((), ())),
            preferred_element_type=jnp.float32,
        )
        total = product if total is None else total + product
    rows = total.shape[0] // 3
    return total[:rows] + total[rows : 2 * rows] + total[2 * rows :]


def kernel(
    G, S, R, main_heads, guide_heads,
    step_ref, main_q, main_k, main_v, guide_q, guide_k, guide_v,
    main_mod, guide_mod, main_head, guide_head, latents,
    velocity, advanced,
    keys, queries, values, weights, sums, attended, final,
    main_table, guide_table, main_weight, guide_weight, held_latents,
    table_sem, recv, send, o_recv, o_send,
):
    g = lax.axis_index("grp")
    s = lax.axis_index("seq")
    rows = main_q.shape[1]
    block = guide_q.shape[1]
    tokens = keys.shape[0]
    count = queries.shape[0]
    blocks = count // block
    heads = main_heads + guide_heads
    half = SLOTS // 2
    unit = (s + 2 * R * g * (S - 1)) % S
    slot = unit // R
    part = unit % R
    head_here = slot // 2 + half * (slot % 2)

    tables = (
        (main_mod, main_table), (guide_mod, guide_table),
        (main_head, main_weight), (guide_head, guide_weight),
        (latents, held_latents),
    )

    barrier = pltpu.get_barrier_semaphore()

    planes = [lax.rem(g + 1 + d, G) for d in range(G)]
    for d in range(G):
        def greet(i, plane=planes[d]):
            pl.semaphore_signal(
                barrier, inc=1, device_id={"grp": plane, "seq": lax.rem(s + 1 + i, S)}
            )

        loop(S if d < G - 1 else S - 1, greet)
    pl.semaphore_wait(barrier, G * S - 1)

    main_sources = (main_k.at[0], main_q.at[0], main_v.at[0])
    guide_sources = (guide_k.at[0], guide_q.at[0], guide_v.at[0])
    targets = (keys, queries, values)
    places = (s * block, lax.rem(s, blocks) * block, s * block)

    def unit_of(head):
        return R * (lax.rem(2 * head, SLOTS) + head // half)

    def send_piece(a, src, dst, plane, first, near):
        def one(r):
            seq = lax.rem(first + r, S)

            def away():
                pltpu.make_async_remote_copy(
                    src_ref=src, dst_ref=dst, send_sem=send, recv_sem=recv.at[a],
                    device_id={"grp": plane, "seq": seq},
                ).start()

            if near:
                @pl.when(seq == s)
                def _():
                    pltpu.make_async_copy(src, dst, recv.at[a]).start()

                pl.when(seq != s)(away)
            else:
                away()

        if a == QUERY:
            one(s // blocks)
        else:
            loop(R, one)

    turns = [lax.rem(s + i, main_heads) for i in range(main_heads)]
    offsets = [unit_of(head) for head in turns]
    shifts = [2 * R * plane for plane in planes]
    for a in range(3):
        dst = targets[a].at[pl.ds(aligned(places[a] + g * rows, rows), rows), :]
        for i in range(main_heads):
            for d in range(G):
                column = (planes[d] * main_heads + turns[i]) * HD
                src = main_sources[a].at[:, pl.ds(aligned(column, HD), HD)]
                send_piece(a, src, dst, planes[d], offsets[i] + shifts[d], d == G - 1)
        dst = targets[a].at[pl.ds(aligned(places[a], block), block), :]
        for head in range(guide_heads):
            src = guide_sources[a].at[:, pl.ds(head * HD, HD)]
            send_piece(a, src, dst, g, unit_of(main_heads + head) + 2 * R * g, True)
    for i, (src, dst) in enumerate(tables):
        pltpu.make_async_copy(src, dst, table_sem.at[i]).start()

    factor = math.log2(math.e) / math.sqrt(HD)
    score_rows = max(32, min(256, 256 * 1024 // tokens))
    value_rows = min(256, count)
    value_blocks = count // value_rows

    @pl.when(head_here < heads)
    def _():
        wait_for(keys, recv.at[KEY])
        wait_for(queries, recv.at[QUERY])

        def score(i):
            at = pl.ds(i * score_rows, score_rows)
            scores = lax.dot_general(
                queries[at, :], keys[...], (((1,), (1,)), ((), ())),
                preferred_element_type=jnp.float32,
            )
            highest = jnp.max(scores, axis=-1, keepdims=True)
            unrounded = jnp.exp2((scores - highest) * factor)
            sums[at, :] = jnp.broadcast_to(
                jnp.sum(unrounded, axis=-1, keepdims=True), (score_rows, HD)
            )
            weights[at, :] = unrounded.astype(jnp.bfloat16)

        loop(count // score_rows, score)
        wait_for(values, recv.at[VALUE])
        column = aligned((g * heads + head_here) * HD, HD)
        for i in range(value_blocks):
            turn = (i + s // 2) % value_blocks
            at = pl.ds(aligned(turn * value_rows, value_rows), value_rows)
            summed = jnp.dot(weights[at, :], values[...], preferred_element_type=jnp.float32)
            attended[at, :] = (summed / sums[at, :]).astype(jnp.bfloat16)
            for b in range(value_rows // block):
                seq = part * blocks + turn * (value_rows // block) + b
                for d in range(G):
                    plane = (g + d + 1) % G
                    first = turn * value_rows + b * block + plane * rows
                    src = attended.at[pl.ds(aligned(first, rows), rows), :]
                    dst = final.at[:, pl.ds(column, HD)]

                    def send_out():
                        pltpu.make_async_remote_copy(
                            src_ref=src, dst_ref=dst, send_sem=o_send, recv_sem=o_recv,
                            device_id={"grp": plane, "seq": seq},
                        ).start()

                    if d < G - 1:
                        send_out()
                    else:
                        @pl.when(seq == s)
                        def _():
                            pltpu.make_async_copy(src, dst, o_recv).start()

                        pl.when(seq != s)(send_out)

    for i, (src, dst) in enumerate(tables):
        pltpu.make_async_copy(src, dst, table_sem.at[i]).wait()
    step_now = step_ref[0]
    main_row = main_table[step_now].astype(jnp.float32)
    guide_row = guide_table[step_now].astype(jnp.float32)
    wait_for(final, o_recv)

    def taken(first, number):
        return [
            final[:, (i * heads + first) * HD : (i * heads + first + number) * HD].astype(jnp.float32)
            for i in range(G)
        ]

    main_flow = project(taken(0, main_heads), main_row, main_weight)
    guide_flow = project(taken(main_heads, guide_heads), guide_row, guide_weight)
    mixed = guide_flow + guidance * (main_flow - guide_flow)
    index = jnp.full((1, mixed.shape[1]), step_now, jnp.int32)
    velocity[0] = mixed
    advanced[0] = held_latents[0] + (sigma_at(index + 1) - sigma_at(index)) * mixed

    own_part = s // blocks == part
    is_main = head_here < main_heads
    is_guide = (head_here >= main_heads) & (head_here < heads)

    def wait_sent(ref, owned):
        @pl.when(owned)
        def _():
            wait_for(ref.at[:, pl.ds(HD, ref.shape[1] - HD)], send)

        @pl.when(jnp.logical_not(owned))
        def _():
            wait_for(ref, send)

    for a in range(3):
        if a != QUERY:
            for r in range(R - 1):
                wait_for(main_sources[a], send)
                wait_for(guide_sources[a], send)
        mine = own_part if a == QUERY else True
        wait_sent(main_sources[a], is_main & mine)
        wait_sent(guide_sources[a], is_guide & mine)

    @pl.when(head_here < heads)
    def _():
        wait_for(attended.at[pl.ds(0, count - rows), :], o_send)

        @pl.when(jnp.logical_not(own_part))
        def _():
            wait_for(attended.at[pl.ds(0, rows), :], o_send)


def on_device(G, S, *arguments):
    (main_query, main_key, main_value, guide_query, guide_key, guide_value,
     latents, step_index, main_mod, guide_mod, main_head, guide_head) = arguments
    R = max(1, S // SLOTS)
    main_heads = HM // G
    guide_heads = guide_query.shape[2] // HD
    heads = main_heads + guide_heads
    rows = main_query.shape[1]
    block = guide_query.shape[1]
    tokens = S * block
    count = tokens // R
    bf16 = jnp.bfloat16
    anywhere = pl.BlockSpec(memory_space=pltpu.HBM)
    vmem = pl.BlockSpec(memory_space=pltpu.VMEM)
    dma = pltpu.SemaphoreType.DMA
    return pl.pallas_call(
        functools.partial(kernel, G, S, R, main_heads, guide_heads),
        out_shape=[jax.ShapeDtypeStruct(latents.shape, jnp.float32)] * 2,
        in_specs=[pl.BlockSpec(memory_space=pltpu.SMEM)] + [anywhere] * 11,
        out_specs=[vmem, vmem],
        scratch_shapes=[
            pltpu.VMEM((tokens, HD), bf16),
            pltpu.VMEM((count, HD), bf16),
            pltpu.VMEM((tokens, HD), bf16),
            pltpu.VMEM((count, tokens), bf16),
            pltpu.VMEM((count, HD), jnp.float32),
            pltpu.VMEM((count, HD), bf16),
            pltpu.VMEM((rows, G * heads * HD), bf16),
            pltpu.VMEM(main_mod.shape, bf16),
            pltpu.VMEM(guide_mod.shape, bf16),
            pltpu.VMEM(main_head.shape[::-1], bf16),
            pltpu.VMEM(guide_head.shape[::-1], bf16),
            pltpu.VMEM(latents.shape, jnp.float32),
            dma((5,)), dma((3,)), dma, dma, dma,
        ],
        compiler_params=pltpu.CompilerParams(
            collective_id=0, has_side_effects=True, vmem_limit_bytes=60 * 1024 * 1024
        ),
        cost_estimate=pl.CostEstimate(
            flops=4 * count * tokens * HD, bytes_accessed=4 * tokens * HD * 2,
            transcendentals=count * tokens,
        ),
    )(
        step_index, main_query, main_key, main_value, guide_query, guide_key, guide_value,
        main_mod, guide_mod, main_head.T, guide_head.T, latents,
    )


def solution(mesh):
    return jax.shard_map(
        functools.partial(on_device, mesh.shape["grp"], mesh.shape["seq"]),
        mesh=mesh,
        in_specs=(
            P("seq", "grp", None),
            P("seq", "grp", None),
            P("seq", "grp", None),
            P("seq", None, "grp"),
            P("seq", None, "grp"),
            P("seq", None, "grp"),
            P("seq", "grp", None),
            P(),
            P(),
            P(),
            P(),
            P(),
        ),
        out_specs=(P("seq", "grp", None), P("seq", "grp", None)),
        check_vma=False,
    )
```

```python
import functools
import math

import jax
import jax.numpy as jnp
from jax import lax
from jax.experimental import pallas as pl
from jax.experimental.pallas import tpu as pltpu
from jax.sharding import PartitionSpec as P

HD = 128
HM = 20
STEPS = 50
SLOTS = 8

guidance = 2.5
flow_shift = 3.0
epsilon = 1e-06

KEY, QUERY, VALUE = 0, 1, 2


def sigma_at(index):
    remaining = 1.0 - index.astype(jnp.float32) / STEPS
    return flow_shift * remaining / (1.0 + (flow_shift - 1.0) * remaining)


def aligned(value, multiple):
    return pl.multiple_of(value, multiple)


def wait_for(ref, sem):
    pltpu.make_async_copy(ref, ref, sem).wait()


def loop(count, body):
    if count <= 8:
        for i in range(count):
            body(i)
    else:
        pl.loop(0, count)(body)


def project(pieces, row, weight_ref):
    width = sum(piece.shape[1] for piece in pieces)
    center = sum(jnp.sum(piece, axis=-1, keepdims=True) for piece in pieces) * (1.0 / width)
    centered = [piece - center for piece in pieces]
    spread = sum(jnp.sum(piece * piece, axis=-1, keepdims=True) for piece in centered) * (1.0 / width)
    scale = lax.rsqrt(spread + epsilon)
    total = None
    start = 0
    for piece in centered:
        part = slice(start, start + piece.shape[1])
        start += piece.shape[1]
        wide = piece * scale * (1.0 + row[1:2, part]) + row[0:1, part]
        high = wide.astype(jnp.bfloat16)
        rest = wide - high.astype(jnp.float32)
        middle = rest.astype(jnp.bfloat16)
        low = (rest - middle.astype(jnp.float32)).astype(jnp.bfloat16)
        product = lax.dot_general(
            jnp.concatenate([high, middle, low], axis=0),
            weight_ref[:, part],
            (((1,), (1,)), ((), ())),
            preferred_element_type=jnp.float32,
        )
        total = product if total is None else total + product
    rows = total.shape[0] // 3
    return total[:rows] + total[rows : 2 * rows] + total[2 * rows :]


def kernel(
    G, S, R, main_heads, guide_heads,
    step_ref, main_q, main_k, main_v, guide_q, guide_k, guide_v,
    main_mod, guide_mod, main_head, guide_head, latents,
    result,
    keys, queries, values, weights, sums, attended, final,
    main_table, guide_table, main_weight, guide_weight, held_latents,
    table_sem, recv, send, o_recv, o_send,
):
    g = lax.axis_index("grp")
    s = lax.axis_index("seq")
    rows = main_q.shape[1]
    block = guide_q.shape[1]
    tokens = keys.shape[0]
    count = queries.shape[0]
    blocks = count // block
    heads = main_heads + guide_heads
    half = SLOTS // 2
    unit = (s + 2 * R * g * (S - 1)) % S
    slot = unit // R
    part = unit % R
    head_here = slot // 2 + half * (slot % 2)

    tables = (
        (main_mod, main_table), (guide_mod, guide_table),
        (main_head, main_weight), (guide_head, guide_weight),
        (latents, held_latents),
    )

    barrier = pltpu.get_barrier_semaphore()

    planes = [lax.rem(g + 1 + d, G) for d in range(G)]
    for d in range(G):
        def greet(i, plane=planes[d]):
            pl.semaphore_signal(
                barrier, inc=1, device_id={"grp": plane, "seq": lax.rem(s + 1 + i, S)}
            )

        loop(S if d < G - 1 else S - 1, greet)
    pl.semaphore_wait(barrier, G * S - 1)

    main_sources = (main_k.at[0], main_q.at[0], main_v.at[0])
    guide_sources = (guide_k.at[0], guide_q.at[0], guide_v.at[0])
    targets = (keys, queries, values)
    places = (s * block, lax.rem(s, blocks) * block, s * block)

    def unit_of(head):
        return R * (lax.rem(2 * head, SLOTS) + head // half)

    def send_piece(a, src, dst, plane, first, near):
        def one(r):
            seq = lax.rem(first + r, S)

            def away():
                pltpu.make_async_remote_copy(
                    src_ref=src, dst_ref=dst, send_sem=send.at[a], recv_sem=recv.at[a],
                    device_id={"grp": plane, "seq": seq},
                ).start()

            if near:
                @pl.when(seq == s)
                def _():
                    pltpu.make_async_copy(src, dst, recv.at[a]).start()

                pl.when(seq != s)(away)
            else:
                away()

        if a == QUERY:
            one(s // blocks)
        else:
            loop(R, one)

    own_part = s // blocks == part
    is_main = head_here < main_heads
    is_guide = (head_here >= main_heads) & (head_here < heads)

    def wait_but_own(ref, owned, sem):
        @pl.when(owned)
        def _():
            wait_for(ref.at[:, pl.ds(HD, ref.shape[1] - HD)], sem)

        @pl.when(jnp.logical_not(owned))
        def _():
            wait_for(ref, sem)

    def wait_sent(a):
        if a != QUERY:
            for r in range(R - 1):
                wait_for(main_sources[a], send.at[a])
                wait_for(guide_sources[a], send.at[a])
        mine = own_part if a == QUERY else True
        wait_but_own(main_sources[a], is_main & mine, send.at[a])
        wait_but_own(guide_sources[a], is_guide & mine, send.at[a])

    turns = [lax.rem(s + i, main_heads) for i in range(main_heads)]
    offsets = [unit_of(head) for head in turns]
    shifts = [2 * R * plane for plane in planes]
    for a in range(3):
        if a == VALUE:
            wait_sent(KEY)
        dst = targets[a].at[pl.ds(aligned(places[a] + g * rows, rows), rows), :]
        for i in range(main_heads):
            for d in range(G):
                column = (planes[d] * main_heads + turns[i]) * HD
                src = main_sources[a].at[:, pl.ds(aligned(column, HD), HD)]
                send_piece(a, src, dst, planes[d], offsets[i] + shifts[d], d == G - 1)
        dst = targets[a].at[pl.ds(aligned(places[a], block), block), :]
        for head in range(guide_heads):
            src = guide_sources[a].at[:, pl.ds(head * HD, HD)]
            send_piece(a, src, dst, g, unit_of(main_heads + head) + 2 * R * g, True)
    for i, (src, dst) in enumerate(tables):
        pltpu.make_async_copy(src, dst, table_sem.at[i]).start()

    factor = math.log2(math.e) / math.sqrt(HD)
    score_rows = max(32, min(256, 256 * 1024 // tokens))
    value_rows = min(256, count)
    value_blocks = count // value_rows

    @pl.when(head_here < heads)
    def _():
        wait_for(keys, recv.at[KEY])
        wait_for(queries, recv.at[QUERY])

        def score(i):
            at = pl.ds(i * score_rows, score_rows)
            scores = lax.dot_general(
                queries[at, :], keys[...], (((1,), (1,)), ((), ())),
                preferred_element_type=jnp.float32,
            )
            highest = jnp.max(scores, axis=-1, keepdims=True)
            unrounded = jnp.exp2((scores - highest) * factor)
            sums[at, :] = jnp.broadcast_to(
                jnp.sum(unrounded, axis=-1, keepdims=True), (score_rows, HD)
            )
            weights[at, :] = unrounded.astype(jnp.bfloat16)

        loop(count // score_rows, score)
        wait_for(values, recv.at[VALUE])
        column = aligned((g * heads + head_here) * HD, HD)
        for i in range(value_blocks):
            turn = (i + s // 2) % value_blocks
            at = pl.ds(aligned(turn * value_rows, value_rows), value_rows)
            summed = jnp.dot(weights[at, :], values[...], preferred_element_type=jnp.float32)
            attended[at, :] = (summed / sums[at, :]).astype(jnp.bfloat16)
            for b in range(value_rows // block):
                seq = part * blocks + turn * (value_rows // block) + b
                for d in range(G):
                    plane = (g + d + 1) % G
                    first = turn * value_rows + b * block + plane * rows
                    src = attended.at[pl.ds(aligned(first, rows), rows), :]
                    dst = final.at[:, pl.ds(column, HD)]

                    def send_out():
                        pltpu.make_async_remote_copy(
                            src_ref=src, dst_ref=dst, send_sem=o_send, recv_sem=o_recv,
                            device_id={"grp": plane, "seq": seq},
                        ).start()

                    if d < G - 1:
                        send_out()
                    else:
                        @pl.when(seq == s)
                        def _():
                            pltpu.make_async_copy(src, dst, o_recv).start()

                        pl.when(seq != s)(send_out)

    for i, (src, dst) in enumerate(tables):
        pltpu.make_async_copy(src, dst, table_sem.at[i]).wait()
    step_now = step_ref[0]
    main_row = main_table[step_now].astype(jnp.float32)
    guide_row = guide_table[step_now].astype(jnp.float32)
    wait_for(final, o_recv)

    def taken(first, number):
        return [
            final[:, (i * heads + first) * HD : (i * heads + first + number) * HD].astype(jnp.float32)
            for i in range(G)
        ]

    main_flow = project(taken(0, main_heads), main_row, main_weight)
    guide_flow = project(taken(main_heads, guide_heads), guide_row, guide_weight)
    mixed = guide_flow + guidance * (main_flow - guide_flow)
    index = jnp.full((1, mixed.shape[1]), step_now, jnp.int32)
    result[0] = mixed
    result[1] = held_latents[0] + (sigma_at(index + 1) - sigma_at(index)) * mixed

    wait_sent(QUERY)
    wait_sent(VALUE)

    @pl.when(head_here < heads)
    def _():
        wait_for(attended.at[pl.ds(0, count - rows), :], o_send)

        @pl.when(jnp.logical_not(own_part))
        def _():
            wait_for(attended.at[pl.ds(0, rows), :], o_send)


def on_device(G, S, *arguments):
    (main_query, main_key, main_value, guide_query, guide_key, guide_value,
     latents, step_index, main_mod, guide_mod, main_head, guide_head) = arguments
    R = max(1, S // SLOTS)
    main_heads = HM // G
    guide_heads = guide_query.shape[2] // HD
    heads = main_heads + guide_heads
    rows = main_query.shape[1]
    block = guide_query.shape[1]
    tokens = S * block
    count = tokens // R
    bf16 = jnp.bfloat16
    anywhere = pl.BlockSpec(memory_space=pltpu.HBM)
    vmem = pl.BlockSpec(memory_space=pltpu.VMEM)
    dma = pltpu.SemaphoreType.DMA
    both = pl.pallas_call(
        functools.partial(kernel, G, S, R, main_heads, guide_heads),
        out_shape=jax.ShapeDtypeStruct((2,) + latents.shape[1:], jnp.float32),
        in_specs=[pl.BlockSpec(memory_space=pltpu.SMEM)] + [anywhere] * 11,
        out_specs=vmem,
        scratch_shapes=[
            pltpu.VMEM((tokens, HD), bf16),
            pltpu.VMEM((count, HD), bf16),
            pltpu.VMEM((tokens, HD), bf16),
            pltpu.VMEM((count, tokens), bf16),
            pltpu.VMEM((count, HD), jnp.float32),
            pltpu.VMEM((count, HD), bf16),
            pltpu.VMEM((rows, G * heads * HD), bf16),
            pltpu.VMEM(main_mod.shape, bf16),
            pltpu.VMEM(guide_mod.shape, bf16),
            pltpu.VMEM(main_head.shape[::-1], bf16),
            pltpu.VMEM(guide_head.shape[::-1], bf16),
            pltpu.VMEM(latents.shape, jnp.float32),
            dma((5,)), dma((3,)), dma((3,)), dma, dma,
        ],
        compiler_params=pltpu.CompilerParams(
            collective_id=0, has_side_effects=True, vmem_limit_bytes=60 * 1024 * 1024
        ),
        cost_estimate=pl.CostEstimate(
            flops=4 * count * tokens * HD, bytes_accessed=4 * tokens * HD * 2,
            transcendentals=count * tokens,
        ),
    )(
        step_index, main_query, main_key, main_value, guide_query, guide_key, guide_value,
        main_mod, guide_mod, main_head.T, guide_head.T, latents,
    )
    return both[:1], both[1:]


def solution(mesh):
    return jax.shard_map(
        functools.partial(on_device, mesh.shape["grp"], mesh.shape["seq"]),
        mesh=mesh,
        in_specs=(
            P("seq", "grp", None),
            P("seq", "grp", None),
            P("seq", "grp", None),
            P("seq", None, "grp"),
            P("seq", None, "grp"),
            P("seq", None, "grp"),
            P("seq", "grp", None),
            P(),
            P(),
            P(),
            P(),
            P(),
        ),
        out_specs=(P("seq", "grp", None), P("seq", "grp", None)),
        check_vma=False,
    )
```

```python
import functools
import math

import jax
import jax.numpy as jnp
from jax import lax
from jax.experimental import pallas as pl
from jax.experimental.pallas import tpu as pltpu
from jax.sharding import PartitionSpec as P

HD = 128
HM = 20
STEPS = 50
SLOTS = 8

guidance = 2.5
flow_shift = 3.0
epsilon = 1e-06

KEY, QUERY, VALUE = 0, 1, 2


def sigma_at(index):
    remaining = 1.0 - index.astype(jnp.float32) / STEPS
    return flow_shift * remaining / (1.0 + (flow_shift - 1.0) * remaining)


def aligned(value, multiple):
    return pl.multiple_of(value, multiple)


def wait_for(ref, sem):
    pltpu.make_async_copy(ref, ref, sem).wait()


def loop(count, body):
    if count <= 8:
        for i in range(count):
            body(i)
    else:
        pl.loop(0, count)(body)


def across(left, right):
    return lax.dot_general(left, right, (((1,), (1,)), ((), ())), preferred_element_type=jnp.float32)


def join(product):
    channels = product.shape[1] // 3
    return product[:, :channels] + product[:, channels : 2 * channels] + product[:, 2 * channels :]


def prepare(row, weight_ref, scaled_ref):
    weight = weight_ref[...]
    wide = weight.astype(jnp.float32) * (1.0 + row[1:2].astype(jnp.float32))
    high = wide.astype(jnp.bfloat16)
    rest = wide - high.astype(jnp.float32)
    middle = rest.astype(jnp.bfloat16)
    low = (rest - middle.astype(jnp.float32)).astype(jnp.bfloat16)
    scaled_ref[...] = jnp.concatenate([high, middle, low], axis=0)
    column_sum = join(across(jnp.ones((16, weight.shape[1]), jnp.bfloat16), scaled_ref[...]))
    shift = across(jnp.broadcast_to(row[0:1].astype(jnp.float32), (16, weight.shape[1])).astype(jnp.bfloat16), weight)
    return column_sum[0:1], shift[0:1]


def project(pieces, scaled_ref, column_sum, shift):
    width = sum(piece.shape[1] for piece in pieces)
    total = None
    start = 0
    for piece in pieces:
        product = across(piece, scaled_ref[:, start : start + piece.shape[1]])
        start += piece.shape[1]
        total = product if total is None else total + product
    pieces = [piece.astype(jnp.float32) for piece in pieces]
    center = sum(jnp.sum(piece, axis=-1, keepdims=True) for piece in pieces) * (1.0 / width)
    centered = [piece - center for piece in pieces]
    spread = sum(jnp.sum(piece * piece, axis=-1, keepdims=True) for piece in centered) * (1.0 / width)
    return lax.rsqrt(spread + epsilon) * (join(total) - center * column_sum) + shift


def kernel(
    G, S, R, main_heads, guide_heads,
    step_ref, main_q, main_k, main_v, guide_q, guide_k, guide_v,
    main_mod, guide_mod, main_head, guide_head, latents,
    result,
    keys, queries, values, weights, sums, attended, final,
    main_table, guide_table, main_weight, guide_weight, held_latents, held_step,
    main_scaled, guide_scaled,
    table_sem, recv, send, o_recv, o_send,
):
    g = lax.axis_index("grp")
    s = lax.axis_index("seq")
    rows = main_q.shape[1]
    block = guide_q.shape[1]
    tokens = keys.shape[0]
    count = queries.shape[0]
    blocks = count // block
    heads = main_heads + guide_heads
    half = SLOTS // 2
    unit = (s + 2 * R * g * (S - 1)) % S
    slot = unit // R
    part = unit % R
    head_here = slot // 2 + half * (slot % 2)

    tables = (
        (main_mod, main_table), (guide_mod, guide_table),
        (main_head, main_weight), (guide_head, guide_weight),
        (latents, held_latents), (step_ref, held_step),
    )
    for i, (src, dst) in enumerate(tables):
        pltpu.make_async_copy(src, dst, table_sem.at[i]).start()

    barrier = pltpu.get_barrier_semaphore()

    planes = [lax.rem(g + 1 + d, G) for d in range(G)]
    for d in range(G):
        def greet(i, plane=planes[d]):
            pl.semaphore_signal(
                barrier, inc=1, device_id={"grp": plane, "seq": lax.rem(s + 1 + i, S)}
            )

        loop(S if d < G - 1 else S - 1, greet)
    pl.semaphore_wait(barrier, G * S - 1)

    main_sources = (main_k.at[0], main_q.at[0], main_v.at[0])
    guide_sources = (guide_k.at[0], guide_q.at[0], guide_v.at[0])
    targets = (keys, queries, values)
    places = (s * block, lax.rem(s, blocks) * block, s * block)

    def unit_of(head):
        return R * (lax.rem(2 * head, SLOTS) + head // half)

    def send_piece(a, src, dst, plane, first, near):
        def one(r):
            seq = lax.rem(first + r, S)

            def away():
                pltpu.make_async_remote_copy(
                    src_ref=src, dst_ref=dst, send_sem=send.at[a], recv_sem=recv.at[a],
                    device_id={"grp": plane, "seq": seq},
                ).start()

            if near:
                @pl.when(seq == s)
                def _():
                    pltpu.make_async_copy(src, dst, recv.at[a]).start()

                pl.when(seq != s)(away)
            else:
                away()

        if a == QUERY:
            one(s // blocks)
        else:
            loop(R, one)

    own_part = s // blocks == part
    is_main = head_here < main_heads
    is_guide = (head_here >= main_heads) & (head_here < heads)

    def wait_but_own(ref, owned, sem):
        @pl.when(owned)
        def _():
            wait_for(ref.at[:, pl.ds(HD, ref.shape[1] - HD)], sem)

        @pl.when(jnp.logical_not(owned))
        def _():
            wait_for(ref, sem)

    def wait_sent(a):
        if a != QUERY:
            for r in range(R - 1):
                wait_for(main_sources[a], send.at[a])
                wait_for(guide_sources[a], send.at[a])
        mine = own_part if a == QUERY else True
        wait_but_own(main_sources[a], is_main & mine, send.at[a])
        wait_but_own(guide_sources[a], is_guide & mine, send.at[a])

    turns = [lax.rem(s + i, main_heads) for i in range(main_heads)]
    offsets = [unit_of(head) for head in turns]
    shifts = [2 * R * plane for plane in planes]
    for a in range(3):
        if a == VALUE:
            wait_sent(KEY)
        dst = targets[a].at[pl.ds(aligned(places[a] + g * rows, rows), rows), :]
        for i in range(main_heads):
            for d in range(G):
                column = (planes[d] * main_heads + turns[i]) * HD
                src = main_sources[a].at[:, pl.ds(aligned(column, HD), HD)]
                send_piece(a, src, dst, planes[d], offsets[i] + shifts[d], d == G - 1)
        dst = targets[a].at[pl.ds(aligned(places[a], block), block), :]
        for head in range(guide_heads):
            src = guide_sources[a].at[:, pl.ds(head * HD, HD)]
            send_piece(a, src, dst, g, unit_of(main_heads + head) + 2 * R * g, True)
    for i, (src, dst) in enumerate(tables):
        pltpu.make_async_copy(src, dst, table_sem.at[i]).wait()
    step_now = held_step[0]
    main_parts = prepare(main_table[step_now], main_weight, main_scaled)
    guide_parts = prepare(guide_table[step_now], guide_weight, guide_scaled)

    factor = math.log2(math.e) / math.sqrt(HD)
    score_rows = max(32, min(256, 256 * 1024 // tokens))
    value_rows = min(256, count)
    value_blocks = count // value_rows

    @pl.when(head_here < heads)
    def _():
        wait_for(keys, recv.at[KEY])
        wait_for(queries, recv.at[QUERY])

        def score(i):
            at = pl.ds(i * score_rows, score_rows)
            scores = lax.dot_general(
                queries[at, :], keys[...], (((1,), (1,)), ((), ())),
                preferred_element_type=jnp.float32,
            )
            highest = jnp.max(scores, axis=-1, keepdims=True)
            unrounded = jnp.exp2((scores - highest) * factor)
            sums[at, :] = jnp.broadcast_to(
                jnp.sum(unrounded, axis=-1, keepdims=True), (score_rows, HD)
            )
            weights[at, :] = unrounded.astype(jnp.bfloat16)

        loop(count // score_rows, score)
        wait_for(values, recv.at[VALUE])
        column = aligned((g * heads + head_here) * HD, HD)
        for i in range(value_blocks):
            turn = (i + s // 2) % value_blocks
            at = pl.ds(aligned(turn * value_rows, value_rows), value_rows)
            summed = jnp.dot(weights[at, :], values[...], preferred_element_type=jnp.float32)
            attended[at, :] = (summed / sums[at, :]).astype(jnp.bfloat16)
            for b in range(value_rows // block):
                seq = part * blocks + turn * (value_rows // block) + b
                for d in range(G):
                    plane = (g + d + 1) % G
                    first = turn * value_rows + b * block + plane * rows
                    src = attended.at[pl.ds(aligned(first, rows), rows), :]
                    dst = final.at[:, pl.ds(column, HD)]

                    def send_out():
                        pltpu.make_async_remote_copy(
                            src_ref=src, dst_ref=dst, send_sem=o_send, recv_sem=o_recv,
                            device_id={"grp": plane, "seq": seq},
                        ).start()

                    if d < G - 1:
                        send_out()
                    else:
                        @pl.when(seq == s)
                        def _():
                            pltpu.make_async_copy(src, dst, o_recv).start()

                        pl.when(seq != s)(send_out)

    wait_for(final, o_recv)

    def taken(first, number):
        return [
            final[:, (i * heads + first) * HD : (i * heads + first + number) * HD]
            for i in range(G)
        ]

    main_flow = project(taken(0, main_heads), main_scaled, *main_parts)
    guide_flow = project(taken(main_heads, guide_heads), guide_scaled, *guide_parts)
    mixed = guide_flow + guidance * (main_flow - guide_flow)
    index = jnp.full((1, mixed.shape[1]), step_now, jnp.int32)
    result[0] = mixed
    result[1] = held_latents[0] + (sigma_at(index + 1) - sigma_at(index)) * mixed

    wait_sent(QUERY)
    wait_sent(VALUE)

    @pl.when(head_here < heads)
    def _():
        wait_for(attended.at[pl.ds(0, count - rows), :], o_send)

        @pl.when(jnp.logical_not(own_part))
        def _():
            wait_for(attended.at[pl.ds(0, rows), :], o_send)


def on_device(G, S, *arguments):
    (main_query, main_key, main_value, guide_query, guide_key, guide_value,
     latents, step_index, main_mod, guide_mod, main_head, guide_head) = arguments
    R = max(1, S // SLOTS)
    main_heads = HM // G
    guide_heads = guide_query.shape[2] // HD
    heads = main_heads + guide_heads
    rows = main_query.shape[1]
    block = guide_query.shape[1]
    tokens = S * block
    count = tokens // R
    bf16 = jnp.bfloat16
    anywhere = pl.BlockSpec(memory_space=pltpu.HBM)
    vmem = pl.BlockSpec(memory_space=pltpu.VMEM)
    dma = pltpu.SemaphoreType.DMA
    both = pl.pallas_call(
        functools.partial(kernel, G, S, R, main_heads, guide_heads),
        out_shape=jax.ShapeDtypeStruct((2,) + latents.shape[1:], jnp.float32),
        in_specs=[anywhere] * 12,
        out_specs=vmem,
        scratch_shapes=[
            pltpu.VMEM((tokens, HD), bf16),
            pltpu.VMEM((count, HD), bf16),
            pltpu.VMEM((tokens, HD), bf16),
            pltpu.VMEM((count, tokens), bf16),
            pltpu.VMEM((count, HD), jnp.float32),
            pltpu.VMEM((count, HD), bf16),
            pltpu.VMEM((rows, G * heads * HD), bf16),
            pltpu.VMEM(main_mod.shape, bf16),
            pltpu.VMEM(guide_mod.shape, bf16),
            pltpu.VMEM(main_head.shape[::-1], bf16),
            pltpu.VMEM(guide_head.shape[::-1], bf16),
            pltpu.VMEM(latents.shape, jnp.float32),
            pltpu.SMEM((1,), jnp.int32),
            pltpu.VMEM((3 * main_head.shape[1], main_head.shape[0]), bf16),
            pltpu.VMEM((3 * guide_head.shape[1], guide_head.shape[0]), bf16),
            dma((6,)), dma((3,)), dma((3,)), dma, dma,
        ],
        compiler_params=pltpu.CompilerParams(
            collective_id=0, has_side_effects=True, vmem_limit_bytes=60 * 1024 * 1024
        ),
        cost_estimate=pl.CostEstimate(
            flops=4 * count * tokens * HD, bytes_accessed=4 * tokens * HD * 2,
            transcendentals=count * tokens,
        ),
    )(
        step_index, main_query, main_key, main_value, guide_query, guide_key, guide_value,
        main_mod, guide_mod, main_head.T, guide_head.T, latents,
    )
    return both[:1], both[1:]


def solution(mesh):
    return jax.shard_map(
        functools.partial(on_device, mesh.shape["grp"], mesh.shape["seq"]),
        mesh=mesh,
        in_specs=(
            P("seq", "grp", None),
            P("seq", "grp", None),
            P("seq", "grp", None),
            P("seq", None, "grp"),
            P("seq", None, "grp"),
            P("seq", None, "grp"),
            P("seq", "grp", None),
            P(),
            P(),
            P(),
            P(),
            P(),
        ),
        out_specs=(P("seq", "grp", None), P("seq", "grp", None)),
        check_vma=False,
    )
```

```python
import functools
import math

import jax
import jax.numpy as jnp
from jax import lax
from jax.experimental import pallas as pl
from jax.experimental.pallas import tpu as pltpu
from jax.sharding import PartitionSpec as P

HD = 128
HM = 20
STEPS = 50
SLOTS = 8

guidance = 2.5
flow_shift = 3.0
epsilon = 1e-06

KEY, QUERY, VALUE = 0, 1, 2


def sigma_at(index):
    remaining = 1.0 - index.astype(jnp.float32) / STEPS
    return flow_shift * remaining / (1.0 + (flow_shift - 1.0) * remaining)


def aligned(value, multiple):
    return pl.multiple_of(value, multiple)


def wait_for(ref, sem):
    pltpu.make_async_copy(ref, ref, sem).wait()


def loop(count, body):
    if count <= 8:
        for i in range(count):
            body(i)
    else:
        pl.loop(0, count)(body)


def across(left, right):
    return lax.dot_general(left, right, (((1,), (1,)), ((), ())), preferred_element_type=jnp.float32)


def join(product):
    channels = product.shape[1] // 3
    return product[:, :channels] + product[:, channels : 2 * channels] + product[:, 2 * channels :]


def prepare(row, weight_ref, scaled_ref):
    weight = weight_ref[...]
    wide = weight.astype(jnp.float32) * (1.0 + row[1:2].astype(jnp.float32))
    high = wide.astype(jnp.bfloat16)
    rest = wide - high.astype(jnp.float32)
    middle = rest.astype(jnp.bfloat16)
    low = (rest - middle.astype(jnp.float32)).astype(jnp.bfloat16)
    scaled_ref[...] = jnp.concatenate([high, middle, low], axis=0)
    column_sum = join(across(jnp.ones((16, weight.shape[1]), jnp.bfloat16), scaled_ref[...]))
    shift = across(jnp.broadcast_to(row[0:1].astype(jnp.float32), (16, weight.shape[1])).astype(jnp.bfloat16), weight)
    return column_sum[0:1], shift[0:1]


def project(pieces, scaled_ref, column_sum, shift):
    width = sum(piece.shape[1] for piece in pieces)
    total = None
    start = 0
    for piece in pieces:
        product = across(piece, scaled_ref[:, start : start + piece.shape[1]])
        start += piece.shape[1]
        total = product if total is None else total + product
    pieces = [piece.astype(jnp.float32) for piece in pieces]
    center = sum(jnp.sum(piece, axis=-1, keepdims=True) for piece in pieces) * (1.0 / width)
    centered = [piece - center for piece in pieces]
    spread = sum(jnp.sum(piece * piece, axis=-1, keepdims=True) for piece in centered) * (1.0 / width)
    return lax.rsqrt(spread + epsilon) * (join(total) - center * column_sum) + shift


def kernel(
    G, S, R, main_heads, guide_heads,
    step_ref, main_q, main_k, main_v, guide_q, guide_k, guide_v,
    main_mod, guide_mod, main_head, guide_head, latents,
    result,
    keys, queries, values, weights, sums, attended, final,
    main_table, guide_table, main_weight, guide_weight, held_latents, held_step,
    main_scaled, guide_scaled, scores,
    table_sem, recv, send, o_recv, o_send,
):
    g = lax.axis_index("grp")
    s = lax.axis_index("seq")
    rows = main_q.shape[1]
    block = guide_q.shape[1]
    tokens = keys.shape[0]
    count = queries.shape[0]
    blocks = count // block
    heads = main_heads + guide_heads
    half = SLOTS // 2
    unit = (s + 2 * R * g * (S - 1)) % S
    slot = unit // R
    part = unit % R
    head_here = slot // 2 + half * (slot % 2)

    tables = (
        (main_mod, main_table), (guide_mod, guide_table),
        (main_head, main_weight), (guide_head, guide_weight),
        (latents, held_latents), (step_ref, held_step),
    )
    for i, (src, dst) in enumerate(tables):
        pltpu.make_async_copy(src, dst, table_sem.at[i]).start()

    barrier = pltpu.get_barrier_semaphore()

    planes = [lax.rem(g + 1 + d, G) for d in range(G)]
    for d in range(G):
        def greet(i, plane=planes[d]):
            pl.semaphore_signal(
                barrier, inc=1, device_id={"grp": plane, "seq": lax.rem(s + 1 + i, S)}
            )

        loop(S if d < G - 1 else S - 1, greet)
    pl.semaphore_wait(barrier, G * S - 1)

    main_sources = (main_k.at[0], main_q.at[0], main_v.at[0])
    guide_sources = (guide_k.at[0], guide_q.at[0], guide_v.at[0])
    targets = (keys, queries, values)
    places = (s * block, lax.rem(s, blocks) * block, s * block)

    def unit_of(head):
        return R * (lax.rem(2 * head, SLOTS) + head // half)

    def send_piece(a, src, dst, plane, first, near):
        def one(r):
            seq = lax.rem(first + r, S)

            def away():
                pltpu.make_async_remote_copy(
                    src_ref=src, dst_ref=dst, send_sem=send.at[a], recv_sem=recv.at[a],
                    device_id={"grp": plane, "seq": seq},
                ).start()

            if near:
                @pl.when(seq == s)
                def _():
                    pltpu.make_async_copy(src, dst, recv.at[a]).start()

                pl.when(seq != s)(away)
            else:
                away()

        if a == QUERY:
            one(s // blocks)
        else:
            loop(R, one)

    own_part = s // blocks == part
    is_main = head_here < main_heads
    is_guide = (head_here >= main_heads) & (head_here < heads)

    def wait_but_own(ref, owned, sem):
        @pl.when(owned)
        def _():
            wait_for(ref.at[:, pl.ds(HD, ref.shape[1] - HD)], sem)

        @pl.when(jnp.logical_not(owned))
        def _():
            wait_for(ref, sem)

    def wait_sent(a):
        if a != QUERY:
            for r in range(R - 1):
                wait_for(main_sources[a], send.at[a])
                wait_for(guide_sources[a], send.at[a])
        mine = own_part if a == QUERY else True
        wait_but_own(main_sources[a], is_main & mine, send.at[a])
        wait_but_own(guide_sources[a], is_guide & mine, send.at[a])

    turns = [lax.rem(s + i, main_heads) for i in range(main_heads)]
    offsets = [unit_of(head) for head in turns]
    shifts = [2 * R * plane for plane in planes]
    for a in range(3):
        if a == VALUE:
            wait_sent(KEY)
        dst = targets[a].at[pl.ds(aligned(places[a] + g * rows, rows), rows), :]
        for i in range(main_heads):
            for d in range(G):
                column = (planes[d] * main_heads + turns[i]) * HD
                src = main_sources[a].at[:, pl.ds(aligned(column, HD), HD)]
                send_piece(a, src, dst, planes[d], offsets[i] + shifts[d], d == G - 1)
        dst = targets[a].at[pl.ds(aligned(places[a], block), block), :]
        for head in range(guide_heads):
            src = guide_sources[a].at[:, pl.ds(head * HD, HD)]
            send_piece(a, src, dst, g, unit_of(main_heads + head) + 2 * R * g, True)
    for i, (src, dst) in enumerate(tables):
        pltpu.make_async_copy(src, dst, table_sem.at[i]).wait()
    step_now = held_step[0]
    main_parts = prepare(main_table[step_now], main_weight, main_scaled)
    guide_parts = prepare(guide_table[step_now], guide_weight, guide_scaled)

    factor = math.log2(math.e) / math.sqrt(HD)
    score_rows = max(32, min(256, 256 * 1024 // tokens))
    strip_rows = max(16, min(32, 32 * 1024 // tokens))
    value_rows = min(256, count)
    value_blocks = count // value_rows

    @pl.when(head_here < heads)
    def _():
        wait_for(keys, recv.at[KEY])
        wait_for(queries, recv.at[QUERY])

        def score(i):
            held = scores.at[i % 2]
            held[...] = across(queries[pl.ds(i * score_rows, score_rows), :], keys[...])
            for j in range(score_rows // strip_rows):
                strip = held[pl.ds(j * strip_rows, strip_rows), :]
                highest = jnp.max(strip, axis=-1, keepdims=True)
                unrounded = jnp.exp2((strip - highest) * factor)
                at = pl.ds(i * score_rows + j * strip_rows, strip_rows)
                sums[at, :] = jnp.broadcast_to(
                    jnp.sum(unrounded, axis=-1, keepdims=True), (strip_rows, HD)
                )
                weights[at, :] = unrounded.astype(jnp.bfloat16)

        loop(count // score_rows, score)
        wait_for(values, recv.at[VALUE])
        column = aligned((g * heads + head_here) * HD, HD)
        for i in range(value_blocks):
            turn = (i + s // 2) % value_blocks
            at = pl.ds(aligned(turn * value_rows, value_rows), value_rows)
            summed = jnp.dot(weights[at, :], values[...], preferred_element_type=jnp.float32)
            attended[at, :] = (summed / sums[at, :]).astype(jnp.bfloat16)
            for b in range(value_rows // block):
                seq = part * blocks + turn * (value_rows // block) + b
                for d in range(G):
                    plane = (g + d + 1) % G
                    first = turn * value_rows + b * block + plane * rows
                    src = attended.at[pl.ds(aligned(first, rows), rows), :]
                    dst = final.at[:, pl.ds(column, HD)]

                    def send_out():
                        pltpu.make_async_remote_copy(
                            src_ref=src, dst_ref=dst, send_sem=o_send, recv_sem=o_recv,
                            device_id={"grp": plane, "seq": seq},
                        ).start()

                    if d < G - 1:
                        send_out()
                    else:
                        @pl.when(seq == s)
                        def _():
                            pltpu.make_async_copy(src, dst, o_recv).start()

                        pl.when(seq != s)(send_out)

    wait_for(final, o_recv)

    def taken(first, number):
        return [
            final[:, (i * heads + first) * HD : (i * heads + first + number) * HD]
            for i in range(G)
        ]

    main_flow = project(taken(0, main_heads), main_scaled, *main_parts)
    guide_flow = project(taken(main_heads, guide_heads), guide_scaled, *guide_parts)
    mixed = guide_flow + guidance * (main_flow - guide_flow)
    index = jnp.full((1, mixed.shape[1]), step_now, jnp.int32)
    result[0] = mixed
    result[1] = held_latents[0] + (sigma_at(index + 1) - sigma_at(index)) * mixed

    wait_sent(QUERY)
    wait_sent(VALUE)

    @pl.when(head_here < heads)
    def _():
        wait_for(attended.at[pl.ds(0, count - rows), :], o_send)

        @pl.when(jnp.logical_not(own_part))
        def _():
            wait_for(attended.at[pl.ds(0, rows), :], o_send)


def on_device(G, S, *arguments):
    (main_query, main_key, main_value, guide_query, guide_key, guide_value,
     latents, step_index, main_mod, guide_mod, main_head, guide_head) = arguments
    R = max(1, S // SLOTS)
    main_heads = HM // G
    guide_heads = guide_query.shape[2] // HD
    heads = main_heads + guide_heads
    rows = main_query.shape[1]
    block = guide_query.shape[1]
    tokens = S * block
    count = tokens // R
    bf16 = jnp.bfloat16
    anywhere = pl.BlockSpec(memory_space=pltpu.HBM)
    vmem = pl.BlockSpec(memory_space=pltpu.VMEM)
    dma = pltpu.SemaphoreType.DMA
    both = pl.pallas_call(
        functools.partial(kernel, G, S, R, main_heads, guide_heads),
        out_shape=jax.ShapeDtypeStruct((2,) + latents.shape[1:], jnp.float32),
        in_specs=[anywhere] * 12,
        out_specs=vmem,
        scratch_shapes=[
            pltpu.VMEM((tokens, HD), bf16),
            pltpu.VMEM((count, HD), bf16),
            pltpu.VMEM((tokens, HD), bf16),
            pltpu.VMEM((count, tokens), bf16),
            pltpu.VMEM((count, HD), jnp.float32),
            pltpu.VMEM((count, HD), bf16),
            pltpu.VMEM((rows, G * heads * HD), bf16),
            pltpu.VMEM(main_mod.shape, bf16),
            pltpu.VMEM(guide_mod.shape, bf16),
            pltpu.VMEM(main_head.shape[::-1], bf16),
            pltpu.VMEM(guide_head.shape[::-1], bf16),
            pltpu.VMEM(latents.shape, jnp.float32),
            pltpu.SMEM((1,), jnp.int32),
            pltpu.VMEM((3 * main_head.shape[1], main_head.shape[0]), bf16),
            pltpu.VMEM((3 * guide_head.shape[1], guide_head.shape[0]), bf16),
            pltpu.VMEM((2, max(32, min(256, 256 * 1024 // tokens)), tokens), jnp.float32),
            dma((6,)), dma((3,)), dma((3,)), dma, dma,
        ],
        compiler_params=pltpu.CompilerParams(
            collective_id=0, has_side_effects=True, vmem_limit_bytes=60 * 1024 * 1024
        ),
        cost_estimate=pl.CostEstimate(
            flops=4 * count * tokens * HD, bytes_accessed=4 * tokens * HD * 2,
            transcendentals=count * tokens,
        ),
    )(
        step_index, main_query, main_key, main_value, guide_query, guide_key, guide_value,
        main_mod, guide_mod, main_head.T, guide_head.T, latents,
    )
    return both[:1], both[1:]


def solution(mesh):
    return jax.shard_map(
        functools.partial(on_device, mesh.shape["grp"], mesh.shape["seq"]),
        mesh=mesh,
        in_specs=(
            P("seq", "grp", None),
            P("seq", "grp", None),
            P("seq", "grp", None),
            P("seq", None, "grp"),
            P("seq", None, "grp"),
            P("seq", None, "grp"),
            P("seq", "grp", None),
            P(),
            P(),
            P(),
            P(),
            P(),
        ),
        out_specs=(P("seq", "grp", None), P("seq", "grp", None)),
        check_vma=False,
    )
```

```python
import functools
import math

import jax
import jax.numpy as jnp
from jax import lax
from jax.experimental import pallas as pl
from jax.experimental.pallas import tpu as pltpu
from jax.sharding import PartitionSpec as P

HD = 128
HM = 20
STEPS = 50
SLOTS = 8

guidance = 2.5
flow_shift = 3.0
epsilon = 1e-06

KEY, QUERY, VALUE = 0, 1, 2


def sigma_at(index):
    remaining = 1.0 - index.astype(jnp.float32) / STEPS
    return flow_shift * remaining / (1.0 + (flow_shift - 1.0) * remaining)


def aligned(value, multiple):
    return pl.multiple_of(value, multiple)


def wait_for(ref, sem):
    pltpu.make_async_copy(ref, ref, sem).wait()


def loop(count, body):
    if count <= 8:
        for i in range(count):
            body(i)
    else:
        pl.loop(0, count)(body)


def project(pieces, row, weight_ref):
    width = sum(piece.shape[1] for piece in pieces)
    center = sum(jnp.sum(piece, axis=-1, keepdims=True) for piece in pieces) * (1.0 / width)
    centered = [piece - center for piece in pieces]
    spread = sum(jnp.sum(piece * piece, axis=-1, keepdims=True) for piece in centered) * (1.0 / width)
    scale = lax.rsqrt(spread + epsilon)
    total = None
    start = 0
    for piece in centered:
        part = slice(start, start + piece.shape[1])
        start += piece.shape[1]
        wide = piece * scale * (1.0 + row[1:2, part]) + row[0:1, part]
        high = wide.astype(jnp.bfloat16)
        rest = wide - high.astype(jnp.float32)
        middle = rest.astype(jnp.bfloat16)
        low = (rest - middle.astype(jnp.float32)).astype(jnp.bfloat16)
        product = lax.dot_general(
            jnp.concatenate([high, middle, low], axis=0),
            weight_ref[:, part],
            (((1,), (1,)), ((), ())),
            preferred_element_type=jnp.float32,
        )
        total = product if total is None else total + product
    rows = total.shape[0] // 3
    return total[:rows] + total[rows : 2 * rows] + total[2 * rows :]


def kernel(
    G, S, R, main_heads, guide_heads,
    step_ref, main_q, main_k, main_v, guide_q, guide_k, guide_v,
    main_mod, guide_mod, main_head, guide_head, latents,
    result,
    keys, queries, values, weights, sums, attended, final,
    main_table, guide_table, main_weight, guide_weight, held_latents,
    main_held, guide_held, in_sem, table_sem, recv, send, o_recv, o_send,
):
    g = lax.axis_index("grp")
    s = lax.axis_index("seq")
    rows = main_q.shape[1]
    block = guide_q.shape[1]
    tokens = keys.shape[0]
    count = queries.shape[0]
    blocks = count // block
    heads = main_heads + guide_heads
    half = SLOTS // 2
    unit = (s + 2 * R * g * (S - 1)) % S
    slot = unit // R
    part = unit % R
    head_here = slot // 2 + half * (slot % 2)

    tables = (
        (main_mod, main_table), (guide_mod, guide_table),
        (main_head, main_weight), (guide_head, guide_weight),
        (latents, held_latents),
    )

    inputs = (main_k, main_q, main_v, guide_k, guide_q, guide_v)
    staged = [main_held.at[a] for a in range(3)] + [guide_held.at[a] for a in range(3)]
    arrivals = [
        pltpu.make_async_copy(src.at[0], dst, in_sem.at[i])
        for i, (src, dst) in enumerate(zip(inputs, staged))
    ]
    for a in range(3):
        arrivals[a].start()
        arrivals[3 + a].start()

    barrier = pltpu.get_barrier_semaphore()

    planes = [lax.rem(g + 1 + d, G) for d in range(G)]
    for d in range(G):
        def greet(i, plane=planes[d]):
            pl.semaphore_signal(
                barrier, inc=1, device_id={"grp": plane, "seq": lax.rem(s + 1 + i, S)}
            )

        loop(S if d < G - 1 else S - 1, greet)
    pl.semaphore_wait(barrier, G * S - 1)

    main_sources = staged[:3]
    guide_sources = staged[3:]
    targets = (keys, queries, values)
    places = (s * block, lax.rem(s, blocks) * block, s * block)

    def unit_of(head):
        return R * (lax.rem(2 * head, SLOTS) + head // half)

    def send_piece(a, src, dst, plane, first, near):
        def one(r):
            seq = lax.rem(first + r, S)

            def away():
                pltpu.make_async_remote_copy(
                    src_ref=src, dst_ref=dst, send_sem=send.at[a], recv_sem=recv.at[a],
                    device_id={"grp": plane, "seq": seq},
                ).start()

            if near:
                @pl.when(seq == s)
                def _():
                    pltpu.make_async_copy(src, dst, recv.at[a]).start()

                pl.when(seq != s)(away)
            else:
                away()

        if a == QUERY:
            one(s // blocks)
        else:
            loop(R, one)

    own_part = s // blocks == part
    is_main = head_here < main_heads
    is_guide = (head_here >= main_heads) & (head_here < heads)

    def wait_but_own(ref, owned, sem):
        @pl.when(owned)
        def _():
            wait_for(ref.at[:, pl.ds(HD, ref.shape[1] - HD)], sem)

        @pl.when(jnp.logical_not(owned))
        def _():
            wait_for(ref, sem)

    def wait_sent(a):
        if a != QUERY:
            for r in range(R - 1):
                wait_for(main_sources[a], send.at[a])
                wait_for(guide_sources[a], send.at[a])
        mine = own_part if a == QUERY else True
        wait_but_own(main_sources[a], is_main & mine, send.at[a])
        wait_but_own(guide_sources[a], is_guide & mine, send.at[a])

    turns = [lax.rem(s + i, main_heads) for i in range(main_heads)]
    offsets = [unit_of(head) for head in turns]
    shifts = [2 * R * plane for plane in planes]
    for a in range(3):
        if a == VALUE:
            wait_sent(KEY)
        arrivals[a].wait()
        arrivals[3 + a].wait()
        dst = targets[a].at[pl.ds(aligned(places[a] + g * rows, rows), rows), :]
        for i in range(main_heads):
            for d in range(G):
                column = (planes[d] * main_heads + turns[i]) * HD
                src = main_sources[a].at[:, pl.ds(aligned(column, HD), HD)]
                send_piece(a, src, dst, planes[d], offsets[i] + shifts[d], d == G - 1)
        dst = targets[a].at[pl.ds(aligned(places[a], block), block), :]
        for head in range(guide_heads):
            src = guide_sources[a].at[:, pl.ds(head * HD, HD)]
            send_piece(a, src, dst, g, unit_of(main_heads + head) + 2 * R * g, True)
    for i, (src, dst) in enumerate(tables):
        pltpu.make_async_copy(src, dst, table_sem.at[i]).start()

    factor = math.log2(math.e) / math.sqrt(HD)
    score_rows = max(32, min(256, 256 * 1024 // tokens))
    value_rows = min(256, count)
    value_blocks = count // value_rows

    @pl.when(head_here < heads)
    def _():
        wait_for(keys, recv.at[KEY])
        wait_for(queries, recv.at[QUERY])

        def score(i):
            at = pl.ds(i * score_rows, score_rows)
            scores = lax.dot_general(
                queries[at, :], keys[...], (((1,), (1,)), ((), ())),
                preferred_element_type=jnp.float32,
            )
            highest = jnp.max(scores, axis=-1, keepdims=True)
            unrounded = jnp.exp2((scores - highest) * factor)
            sums[at, :] = jnp.broadcast_to(
                jnp.sum(unrounded, axis=-1, keepdims=True), (score_rows, HD)
            )
            weights[at, :] = unrounded.astype(jnp.bfloat16)

        loop(count // score_rows, score)
        wait_for(values, recv.at[VALUE])
        column = aligned((g * heads + head_here) * HD, HD)
        for i in range(value_blocks):
            turn = (i + s // 2) % value_blocks
            at = pl.ds(aligned(turn * value_rows, value_rows), value_rows)
            summed = jnp.dot(weights[at, :], values[...], preferred_element_type=jnp.float32)
            attended[at, :] = (summed / sums[at, :]).astype(jnp.bfloat16)
            for b in range(value_rows // block):
                seq = part * blocks + turn * (value_rows // block) + b
                for d in range(G):
                    plane = (g + d + 1) % G
                    first = turn * value_rows + b * block + plane * rows
                    src = attended.at[pl.ds(aligned(first, rows), rows), :]
                    dst = final.at[:, pl.ds(column, HD)]

                    def send_out():
                        pltpu.make_async_remote_copy(
                            src_ref=src, dst_ref=dst, send_sem=o_send, recv_sem=o_recv,
                            device_id={"grp": plane, "seq": seq},
                        ).start()

                    if d < G - 1:
                        send_out()
                    else:
                        @pl.when(seq == s)
                        def _():
                            pltpu.make_async_copy(src, dst, o_recv).start()

                        pl.when(seq != s)(send_out)

    for i, (src, dst) in enumerate(tables):
        pltpu.make_async_copy(src, dst, table_sem.at[i]).wait()
    step_now = step_ref[0]
    main_row = main_table[step_now].astype(jnp.float32)
    guide_row = guide_table[step_now].astype(jnp.float32)
    wait_for(final, o_recv)

    def taken(first, number):
        return [
            final[:, (i * heads + first) * HD : (i * heads + first + number) * HD].astype(jnp.float32)
            for i in range(G)
        ]

    main_flow = project(taken(0, main_heads), main_row, main_weight)
    guide_flow = project(taken(main_heads, guide_heads), guide_row, guide_weight)
    mixed = guide_flow + guidance * (main_flow - guide_flow)
    index = jnp.full((1, mixed.shape[1]), step_now, jnp.int32)
    result[0] = mixed
    result[1] = held_latents[0] + (sigma_at(index + 1) - sigma_at(index)) * mixed

    wait_sent(QUERY)
    wait_sent(VALUE)

    @pl.when(head_here < heads)
    def _():
        wait_for(attended.at[pl.ds(0, count - rows), :], o_send)

        @pl.when(jnp.logical_not(own_part))
        def _():
            wait_for(attended.at[pl.ds(0, rows), :], o_send)


def on_device(G, S, *arguments):
    (main_query, main_key, main_value, guide_query, guide_key, guide_value,
     latents, step_index, main_mod, guide_mod, main_head, guide_head) = arguments
    R = max(1, S // SLOTS)
    main_heads = HM // G
    guide_heads = guide_query.shape[2] // HD
    heads = main_heads + guide_heads
    rows = main_query.shape[1]
    block = guide_query.shape[1]
    tokens = S * block
    count = tokens // R
    bf16 = jnp.bfloat16
    anywhere = pl.BlockSpec(memory_space=pltpu.HBM)
    vmem = pl.BlockSpec(memory_space=pltpu.VMEM)
    dma = pltpu.SemaphoreType.DMA
    both = pl.pallas_call(
        functools.partial(kernel, G, S, R, main_heads, guide_heads),
        out_shape=jax.ShapeDtypeStruct((2,) + latents.shape[1:], jnp.float32),
        in_specs=[pl.BlockSpec(memory_space=pltpu.SMEM)] + [anywhere] * 11,
        out_specs=vmem,
        scratch_shapes=[
            pltpu.VMEM((tokens, HD), bf16),
            pltpu.VMEM((count, HD), bf16),
            pltpu.VMEM((tokens, HD), bf16),
            pltpu.VMEM((count, tokens), bf16),
            pltpu.VMEM((count, HD), jnp.float32),
            pltpu.VMEM((count, HD), bf16),
            pltpu.VMEM((rows, G * heads * HD), bf16),
            pltpu.VMEM(main_mod.shape, bf16),
            pltpu.VMEM(guide_mod.shape, bf16),
            pltpu.VMEM(main_head.shape[::-1], bf16),
            pltpu.VMEM(guide_head.shape[::-1], bf16),
            pltpu.VMEM(latents.shape, jnp.float32),
            pltpu.VMEM((3,) + main_query.shape[1:], bf16),
            pltpu.VMEM((3,) + guide_query.shape[1:], bf16),
            dma((6,)), dma((5,)), dma((3,)), dma((3,)), dma, dma,
        ],
        compiler_params=pltpu.CompilerParams(
            collective_id=0, has_side_effects=True, vmem_limit_bytes=60 * 1024 * 1024
        ),
        cost_estimate=pl.CostEstimate(
            flops=4 * count * tokens * HD, bytes_accessed=4 * tokens * HD * 2,
            transcendentals=count * tokens,
        ),
    )(
        step_index, main_query, main_key, main_value, guide_query, guide_key, guide_value,
        main_mod, guide_mod, main_head.T, guide_head.T, latents,
    )
    return both[:1], both[1:]


def solution(mesh):
    return jax.shard_map(
        functools.partial(on_device, mesh.shape["grp"], mesh.shape["seq"]),
        mesh=mesh,
        in_specs=(
            P("seq", "grp", None),
            P("seq", "grp", None),
            P("seq", "grp", None),
            P("seq", None, "grp"),
            P("seq", None, "grp"),
            P("seq", None, "grp"),
            P("seq", "grp", None),
            P(),
            P(),
            P(),
            P(),
            P(),
        ),
        out_specs=(P("seq", "grp", None), P("seq", "grp", None)),
        check_vma=False,
    )
```
